128 devices in a mesh: outer: 32 (over z, y, core), inner: 4 (over x).
Axes of the slice: x: 4, y: 4, z: 4, core: 2. Of those that a mesh axis runs over, the one named last changes fastest.
Arguments:
- x_in: bfloat16 [16384, 8192], P(('outer', 'inner')), may hold values from -6 to 6
- gate_in: bfloat16 [16384, 8192], P(('outer', 'inner')), may hold values from -6 to 6
- conv_weight: float32 [4, 8192], replicated, may hold values from -3 to 3
- conv_bias: float32 [8192], replicated, may hold values from -3 to 3
- x_proj: bfloat16 [8192, 288], replicated, may hold values from -0.0625 to 0.0625
- dt_proj: bfloat16 [256, 8192], replicated, may hold values from -0.375 to 0.375
- dt_bias: float32 [8192], replicated, may hold values from -9 to -2
- decay_rates: float32 [16, 8192], replicated, may hold values from 1 to 16
- skip_gain: float32 [8192], replicated, may hold values from 0.5 to 1.5
Outputs:
- gated_out: bfloat16 [16384, 8192], P(('outer', 'inner'))
The draws below stay inside these ranges and needn't reach their ends.
All inputs are finite; a program needn't handle non-finite values.
Results may differ from the reference program's by a relative error of at most 0.0085.
Values may be sent and summed in bfloat16 or wider, within the bound.
A program may use at most 192 MiB of HBM per device.

```python
import math
import jax
import jax.numpy as jnp
from jax import lax

E = 8192
N = 16
R = 256
KW = 4
TOKENS = 16384


def level_of(stream_key, shape, cuts, low, high):
    def one(position, parts):
        draws = jax.random.uniform(jax.random.fold_in(jax.random.fold_in(stream_key, 6), position), (parts,), jnp.float32, low / len(cuts), high / len(cuts))
        return jnp.repeat(jnp.exp(draws), shape[position] // parts).reshape((-1,) + (1,) * (len(shape) - position - 1))

    level = one(*cuts[0])
    for cut in cuts[1:]:
        level = level * one(*cut)
    return level


def scatter_about(key, shape, scale, bound, shards=(), kind=jnp.bfloat16):
    level = level_of(key, shape, shards, -0.22, 0.18) if shards else 1.0
    entries = jax.random.normal(key, shape, jnp.float32) * scale * level
    return jnp.minimum(jnp.maximum(entries, -bound), bound).astype(kind)


def setup_inputs(seed: int = 0) -> dict:
    key_list = jax.random.split(jax.random.key(seed), 10)
    x_in = scatter_about(key_list[0], (TOKENS, E), 1.0, 6.0, ((0, 128),))
    gate_in = scatter_about(key_list[1], (TOKENS, E), 1.0, 6.0, ((0, 128),))
    conv_weight = scatter_about(key_list[2], (KW, E), KW ** -0.5, 3.0, (), jnp.float32)
    conv_bias = scatter_about(key_list[3], (E,), 0.5, 3.0, (), jnp.float32)
    x_proj = scatter_about(key_list[4], (E, R + 2 * N), E ** -0.5, 0.0625)
    dt_proj = scatter_about(key_list[5], (R, E), R ** -0.5, 0.375)
    dt_bias = jnp.clip(jax.random.uniform(key_list[6], (E,), jnp.float32, -9.0, -2.0), -9.0, -2.0)
    decay_rates = jnp.clip(jnp.exp(jax.random.uniform(key_list[7], (N, E), jnp.float32, math.log(1.0), math.log(16.0))), 1.0, 16.0)
    skip_gain = jnp.clip(1.0 + 0.1 * jax.random.normal(key_list[8], (E,), jnp.float32), 0.5, 1.5)
    return dict(x_in=x_in, gate_in=gate_in, conv_weight=conv_weight, conv_bias=conv_bias, x_proj=x_proj, dt_proj=dt_proj, dt_bias=dt_bias, decay_rates=decay_rates, skip_gain=skip_gain)


dt_ceiling = 0.25


def reference(x_in, gate_in, conv_weight, conv_bias, x_proj, dt_proj, dt_bias, decay_rates, skip_gain):
    length = x_in.shape[0]
    width = x_in.shape[1]
    taps = conv_weight.shape[0]
    xfloat = x_in.astype(jnp.float32)
    padded = jnp.concatenate([jnp.zeros((taps - 1, width), jnp.float32), xfloat], axis=0)
    conv = conv_bias[None, :]
    for k in range(taps):
        conv = conv + conv_weight[k][None, :] * padded[k:k + length]
    u_act = jax.nn.silu(conv).astype(jnp.bfloat16)
    proj = jnp.dot(u_act, x_proj, preferred_element_type=jnp.float32)
    rank = dt_proj.shape[0]
    states = decay_rates.shape[0]
    dt_low = proj[:, :rank].astype(jnp.bfloat16)
    bmat = proj[:, rank:rank + states]
    cmat = proj[:, rank + states:]
    step_size = jnp.minimum(jax.nn.softplus(jnp.dot(dt_low, dt_proj, preferred_element_type=jnp.float32) + dt_bias[None, :]), dt_ceiling)
    ufloat = u_act.astype(jnp.float32)

    def advance(state, inputs):
        dt_row, u_row, b_row, c_row = inputs
        state = jnp.exp(-dt_row[None, :] * decay_rates) * state + b_row[:, None] * (dt_row * u_row)[None, :]
        return state, jnp.sum(c_row[:, None] * state, axis=0)

    start = jnp.zeros((states, width), jnp.float32)
    final, outputs = lax.scan(advance, start, (step_size, ufloat, bmat, cmat))
    y_full = outputs + skip_gain[None, :] * ufloat
    return (y_full * jax.nn.silu(gate_in.astype(jnp.float32))).astype(jnp.bfloat16)
```

```python
import functools
import math

import jax
import jax.numpy as jnp
from jax import lax
from jax.experimental import pallas as pl
from jax.experimental.pallas import tpu as pltpu
from jax.sharding import PartitionSpec as P

f32, bf16 = jnp.float32, jnp.bfloat16
MESH = pl.DeviceIdType.MESH
LOG2E = math.log2(math.e)
LN2 = math.log(2.0)
DT_CEILING = 0.25

T = 128
E = 8192
N = 16
R = 256
KW = 4
LANES = 128
J = 8
GW = J * LANES
G = E // GW
ROWS = T * J
AGG = G * N + G


def silu(v):
    d = 1.0 + jnp.exp2(v * -LOG2E)
    r = pl.reciprocal(d, approx=True)
    r = r * (2.0 - d * r)
    return v * r


def softplus_clipped(v):
    z = jnp.exp2(jnp.minimum(v, 0.0) * LOG2E)
    small = z * (1.0 - z * (0.5 - z * (1.0 / 3.0 - 0.25 * z)))
    big = jnp.log2(1.0 + z) * LN2
    return jnp.minimum(jnp.where(z < 0.03, small, big), DT_CEILING)


def split3(v):
    hi = v.astype(bf16).astype(f32)
    mid = (v - hi).astype(bf16).astype(f32)
    lo = (v - hi - mid).astype(bf16).astype(f32)
    return hi, mid, lo


def scan_kernel(x_hbm, prior_ref, cw_ref, cb_ref, xp_hbm, dp_hbm, db_ref, a_ref,
                y_hbm, c_hbm, u_hbm, cs_hbm, agg_ref,
                x_v, xp_v, dp_v, pad_v, u_v, bs_v, cs_v, ach_v, proj_v, dch_v, ich_v, ych_v, cch_v,
                in_sem, out_sem):
    def x_copy(g):
        return pltpu.make_async_copy(x_hbm.at[:, pl.ds(g * GW, GW)], x_v.at[g], in_sem.at[0, g])

    def xp_copy(g):
        return pltpu.make_async_copy(xp_hbm.at[pl.ds(g * GW, GW), :], xp_v.at[pl.ds(g * GW, GW), :], in_sem.at[1, g])

    def dp_copy(g):
        return pltpu.make_async_copy(dp_hbm.at[:, pl.ds(g * GW, GW)], dp_v.at[g], in_sem.at[2, g])

    for g in range(G):
        x_copy(g).start()
        xp_copy(g).start()
    for g in range(G):
        dp_copy(g).start()

    for q in range(E // LANES):
        g, j = q // J, q % J
        ach_v[g, pl.ds(j, N, stride=J), :] = a_ref[:, q * LANES:(q + 1) * LANES] * -LOG2E

    proj_v[...] = jnp.zeros_like(proj_v)

    def conv_group(g, _):
        off = pl.multiple_of(g * GW, GW)
        x_copy(g).wait()
        pad_v[0:8, :] = prior_ref[:, pl.ds(off, GW)].astype(f32)
        for s in range(0, GW, 256):
            pad_v[8:8 + T, s:s + 256] = x_v[g, :, s:s + 256].astype(f32)
        for s in range(0, GW, LANES):
            w = cw_ref[:, pl.ds(off + s, LANES)]
            acc = cb_ref[:, pl.ds(off + s, LANES)]
            for k in range(KW):
                acc = acc + w[k:k + 1] * pad_v[8 - (KW - 1) + k:8 - (KW - 1) + k + T, s:s + LANES]
            u_v[g, :, s:s + LANES] = silu(acc).astype(bf16)
        xp_copy(g).wait()
        proj_v[...] += jnp.dot(u_v[g], xp_v[pl.ds(off, GW), :], preferred_element_type=f32)
        pltpu.make_async_copy(u_v.at[g], u_hbm.at[g], out_sem.at[2, g]).start()
        return 0

    lax.fori_loop(0, G, conv_group, 0)

    row = lax.broadcasted_iota(jnp.int32, (256, 16), 0)
    col = lax.broadcasted_iota(jnp.int32, (256, 16), 1)
    repeat = (row // N == col).astype(bf16)
    row = lax.broadcasted_iota(jnp.int32, (256, 96), 0)
    col = lax.broadcasted_iota(jnp.int32, (256, 96), 1)
    own = row % N == col % N
    row = lax.broadcasted_iota(jnp.int32, (96, 256), 0)
    col = lax.broadcasted_iota(jnp.int32, (96, 256), 1)
    gather = (row // 48 == col // LANES).astype(bf16)

    def spread(k, _):
        r = pl.multiple_of(k * 16, 16)
        b = proj_v[pl.ds(r, 16), R:R + N]
        c = proj_v[pl.ds(r, 16), R + N:R + 2 * N]
        parts = jnp.concatenate([*split3(b), *split3(c)], axis=1).astype(bf16)
        wide = jnp.dot(repeat, parts, preferred_element_type=f32)
        wide = jnp.where(own, wide, 0.0).astype(bf16)
        full = jnp.dot(wide, gather, preferred_element_type=f32)
        r = pl.multiple_of(k * 256, 256)
        bs_v[pl.ds(r, 256), :] = full[:, :LANES]
        cs_v[pl.ds(r, 256), :] = full[:, LANES:]
        return 0

    lax.fori_loop(0, T // 16, spread, 0)
    cs_copy = pltpu.make_async_copy(cs_v, cs_hbm, out_sem.at[3, 0])
    cs_copy.start()

    def group(g, _):
        off = pl.multiple_of(g * GW, GW)
        dp_copy(g).wait()
        dt_low = proj_v[:, 0:R].astype(bf16)
        for s in range(0, GW, 256):
            v = jnp.dot(dt_low, dp_v[g, :, s:s + 256], preferred_element_type=f32)
            d = softplus_clipped(v + db_ref[:, pl.ds(off + s, 256)])
            i = d * u_v[g, :, s:s + 256].astype(f32)
            for h in range(2):
                j = s // LANES + h
                dch_v[pl.ds(j, T, stride=J), :] = d[:, h * LANES:(h + 1) * LANES]
                ich_v[pl.ds(j, T, stride=J), :] = i[:, h * LANES:(h + 1) * LANES]

        def steps(k, carry):
            h, cum = list(carry[0]), carry[1]
            for tt in range(8):
                t = k * 8 + tt
                r = pl.multiple_of(t * J, J)
                d = dch_v[pl.ds(r, J), :]
                i = ich_v[pl.ds(r, J), :]
                cum = cum + d
                cch_v[g, pl.ds(r, J), :] = cum
                ys = []
                for n in range(N):
                    e = jnp.exp2(d * ach_v[g, n * J:(n + 1) * J, :])
                    b = bs_v[pl.ds(t * N + n, J, stride=0), :]
                    c = cs_v[pl.ds(t * N + n, J, stride=0), :]
                    h[n] = e * h[n] + b * i
                    ys.append(c * h[n])
                    if n % 4 == 3:
                        y4 = (ys[0] + ys[1]) + (ys[2] + ys[3])
                        y = y4 if n == 3 else y + y4
                        ys = []
                ych_v[g, pl.ds(r, J), :] = y
            return tuple(h), cum

        zero = jnp.zeros((J, LANES), f32)
        h, cum = lax.fori_loop(0, T // 8, steps, ((zero,) * N, zero))
        for n in range(N):
            agg_ref[pl.ds(g * N + n, J, stride=AGG), :] = h[n]
        agg_ref[pl.ds(G * N + g, J, stride=AGG), :] = cum
        pltpu.make_async_copy(ych_v.at[g], y_hbm.at[g], out_sem.at[0, g]).start()
        pltpu.make_async_copy(cch_v.at[g], c_hbm.at[g], out_sem.at[1, g]).start()
        return 0

    lax.fori_loop(0, G, group, 0)
    cs_copy.wait()
    for g in range(G):
        pltpu.make_async_copy(ych_v.at[g], y_hbm.at[g], out_sem.at[0, g]).wait()
        pltpu.make_async_copy(cch_v.at[g], c_hbm.at[g], out_sem.at[1, g]).wait()
        pltpu.make_async_copy(u_v.at[g], u_hbm.at[g], out_sem.at[2, g]).wait()


def exchange_kernel(agg_ref, a_ref, carry_ref, got_v, total_v, ys_v, zs_v, in_v, back_v,
                    send1, recv1, sendy, recvy, sendz, recvz, send4, recv4, own_sem):
    outer, x = lax.axis_index("outer"), lax.axis_index("inner")
    core, y, z = outer % 2, (outer // 2) % 4, outer // 8
    me = core * 4 + x

    def member(m):
        return ((z * 4 + y) * 2 + m // 4, m % 4)

    def at_y(v):
        return ((z * 4 + v) * 2 + core, x)

    def at_z(v):
        return ((v * 4 + y) * 2 + core, x)

    barrier = pltpu.get_barrier_semaphore()
    for r in range(1, 8):
        pl.semaphore_signal(barrier, inc=1, device_id=member((me + r) % 8), device_id_type=MESH)
    for r in range(1, 4):
        pl.semaphore_signal(barrier, inc=1, device_id=at_y((y + r) % 4), device_id_type=MESH)
        pl.semaphore_signal(barrier, inc=1, device_id=at_z((z + r) % 4), device_id_type=MESH)
    pl.semaphore_wait(barrier, 13)

    own = pltpu.make_async_copy(agg_ref.at[me], got_v.at[me], own_sem)
    own.start()
    first = []
    for r in range(1, 8):
        to = (me + r) % 8
        cp = pltpu.make_async_remote_copy(
            src_ref=agg_ref.at[to], dst_ref=got_v.at[me], send_sem=send1.at[r], recv_sem=recv1.at[r],
            device_id=member(to), device_id_type=MESH)
        cp.start()
        first.append(cp)
    own.wait()
    for cp in first:
        cp.wait()

    def rates(g):
        return a_ref[:, pl.ds(pl.multiple_of(g * GW + me * LANES, LANES), LANES)] * -LOG2E

    def advance(state, block, g):
        d = block[pl.ds(G * N + g, N, stride=0), :]
        return jnp.exp2(d * rates(g)) * state + block[pl.ds(g * N, N), :]

    dsum = got_v[0, G * N:AGG, :]
    for k in range(1, 8):
        dsum = dsum + got_v[k, G * N:AGG, :]
    total_v[G * N:AGG, :] = dsum
    for g in range(G):
        s = got_v[0, g * N:(g + 1) * N, :]
        for k in range(1, 8):
            s = advance(s, got_v.at[k], g)
        total_v[g * N:(g + 1) * N, :] = s

    def along(source, slots, here, place, send, recv):
        copies = []
        for r in range(1, 4):
            to = (here + r) % 4
            cp = pltpu.make_async_remote_copy(
                src_ref=source, dst_ref=slots.at[here], send_sem=send.at[r], recv_sem=recv.at[r],
                device_id=place(to), device_id_type=MESH)
            cp.start()
            copies.append(cp)
        slots[pl.ds(here, 1)] = source[...][None]
        for cp in copies:
            cp.wait()

    along(total_v, ys_v, y, at_y, sendy, recvy)
    dsum = ys_v[0, G * N:AGG, :]
    dpre = jnp.where(y > 0, dsum, 0.0)
    for k in range(1, 4):
        dpre = dpre + jnp.where(y > k, ys_v[k, G * N:AGG, :], 0.0)
        dsum = dsum + ys_v[k, G * N:AGG, :]
    in_v[G * N:AGG, :] = dpre
    total_v[G * N:AGG, :] = dsum
    for g in range(G):
        s = ys_v[0, g * N:(g + 1) * N, :]
        pre = jnp.where(y > 0, s, 0.0)
        for k in range(1, 4):
            s = advance(s, ys_v.at[k], g)
            pre = jnp.where(y > k, s, pre)
        in_v[g * N:(g + 1) * N, :] = pre
        total_v[g * N:(g + 1) * N, :] = s

    along(total_v, zs_v, z, at_z, sendz, recvz)
    for g in range(G):
        s = zs_v[0, g * N:(g + 1) * N, :]
        pre = jnp.where(z > 0, s, 0.0)
        for k in range(1, 3):
            s = advance(s, zs_v.at[k], g)
            pre = jnp.where(z > k, s, pre)
        s = advance(pre, in_v, g)
        for k in range(8):
            back_v[k, g * N:(g + 1) * N, :] = s
            if k < 7:
                s = advance(s, got_v.at[k], g)

    own = pltpu.make_async_copy(back_v.at[me], carry_ref.at[me], own_sem)
    own.start()
    last = []
    for r in range(1, 8):
        to = (me + r) % 8
        cp = pltpu.make_async_remote_copy(
            src_ref=back_v.at[to], dst_ref=carry_ref.at[me], send_sem=send4.at[r], recv_sem=recv4.at[r],
            device_id=member(to), device_id_type=MESH)
        cp.start()
        last.append(cp)
    own.wait()
    for cp in last:
        cp.wait()


def finish_kernel(y_hbm, c_hbm, u_hbm, cs_hbm, gate_hbm, carry_ref, a_ref, skip_ref,
                  out_hbm, y_v, c_v, u_v, cs_v, gate_v, ach_v, hch_v, out_v, in_sem, out_sem):
    def copies(g):
        cols = pl.ds(pl.multiple_of(g * GW, GW), GW)
        return (pltpu.make_async_copy(y_hbm.at[g], y_v.at[g], in_sem.at[0, g]),
                pltpu.make_async_copy(c_hbm.at[g], c_v.at[g], in_sem.at[1, g]),
                pltpu.make_async_copy(u_hbm.at[g], u_v.at[g], in_sem.at[2, g]),
                pltpu.make_async_copy(gate_hbm.at[:, cols], gate_v.at[g], in_sem.at[3, g]))

    def out_copy(g):
        cols = pl.ds(pl.multiple_of(g * GW, GW), GW)
        return pltpu.make_async_copy(out_v.at[g], out_hbm.at[:, cols], out_sem.at[g])

    cs_copy = pltpu.make_async_copy(cs_hbm, cs_v, in_sem.at[4, 0])
    cs_copy.start()
    for g in range(G):
        for cp in copies(g):
            cp.start()
    for q in range(E // LANES):
        g, j = q // J, q % J
        ach_v[g, pl.ds(j, N, stride=J), :] = a_ref[:, q * LANES:(q + 1) * LANES] * -LOG2E
    cs_copy.wait()

    def group(g, _):
        off = pl.multiple_of(g * GW, GW)
        for cp in copies(g):
            cp.wait()
        for n in range(N):
            hch_v[n * J:(n + 1) * J, :] = carry_ref[pl.ds(g * N + n, J, stride=G * N), :]

        def steps(k, _):
            for tt in range(8):
                t = k * 8 + tt
                r = pl.multiple_of(t * J, J)
                cum = c_v[g, pl.ds(r, J), :]
                y = y_v[g, pl.ds(r, J), :]
                for n4 in range(0, N, 4):
                    part = []
                    for n in range(n4, n4 + 4):
                        e = jnp.exp2(cum * ach_v[g, n * J:(n + 1) * J, :])
                        c = cs_v[pl.ds(t * N + n, J, stride=0), :]
                        part.append(c * (e * hch_v[n * J:(n + 1) * J, :]))
                    y = y + ((part[0] + part[1]) + (part[2] + part[3]))
                y_v[g, pl.ds(r, J), :] = y
            return 0

        lax.fori_loop(0, T // 8, steps, 0)
        for j in range(J):
            cols = slice(j * LANES, (j + 1) * LANES)
            y = y_v[g, pl.ds(j, T, stride=J), :]
            y = y + skip_ref[:, pl.ds(off + j * LANES, LANES)] * u_v[g, :, cols].astype(f32)
            out_v[g, :, cols] = (y * silu(gate_v[g, :, cols].astype(f32))).astype(bf16)
        out_copy(g).start()
        return 0

    lax.fori_loop(0, G, group, 0)
    for g in range(G):
        out_copy(g).wait()


ANY = pl.BlockSpec(memory_space=pl.ANY)
VMEM = pl.BlockSpec(memory_space=pltpu.VMEM)
VMEM_BYTES = 56 * 2**20


def local(x_in, gate_in, conv_weight, conv_bias, x_proj, dt_proj, dt_bias, decay_rates, skip_gain):
    sds = jax.ShapeDtypeStruct
    devices = lax.axis_size("outer") * lax.axis_size("inner")
    prior = lax.ppermute(x_in[T - 8:], ("outer", "inner"), [(s, s + 1) for s in range(devices - 1)])
    y, c, u, cs, agg = pl.pallas_call(
        scan_kernel,
        name="local_scan",
        out_shape=[sds((G, ROWS, LANES), f32), sds((G, ROWS, LANES), f32), sds((G, T, GW), bf16),
                   sds((T * N, LANES), f32), sds((J * AGG, LANES), f32)],
        in_specs=[ANY, VMEM, VMEM, VMEM, ANY, ANY, VMEM, VMEM],
        out_specs=[ANY, ANY, ANY, ANY, VMEM],
        scratch_shapes=[
            pltpu.VMEM((G, T, GW), bf16), pltpu.VMEM((E, R + 2 * N), bf16), pltpu.VMEM((G, R, GW), bf16),
            pltpu.VMEM((T + 8, GW), f32), pltpu.VMEM((G, T, GW), bf16),
            pltpu.VMEM((T * N, LANES), f32), pltpu.VMEM((T * N, LANES), f32),
            pltpu.VMEM((G, N * J, LANES), f32), pltpu.VMEM((T, R + 2 * N), f32),
            pltpu.VMEM((ROWS, LANES), f32), pltpu.VMEM((ROWS, LANES), f32),
            pltpu.VMEM((G, ROWS, LANES), f32), pltpu.VMEM((G, ROWS, LANES), f32),
            pltpu.SemaphoreType.DMA((3, G)), pltpu.SemaphoreType.DMA((4, G))],
        compiler_params=pltpu.CompilerParams(vmem_limit_bytes=VMEM_BYTES),
    )(x_in, prior, conv_weight, conv_bias.reshape(1, E), x_proj, dt_proj, dt_bias.reshape(1, E), decay_rates)

    carry = pl.pallas_call(
        exchange_kernel,
        name="exchange",
        out_shape=sds((J, G * N, LANES), f32),
        in_specs=[VMEM, VMEM],
        out_specs=VMEM,
        scratch_shapes=[
            pltpu.VMEM((8, AGG, LANES), f32), pltpu.VMEM((AGG, LANES), f32),
            pltpu.VMEM((4, AGG, LANES), f32), pltpu.VMEM((4, AGG, LANES), f32), pltpu.VMEM((AGG, LANES), f32),
            pltpu.VMEM((8, G * N, LANES), f32),
            pltpu.SemaphoreType.DMA((8,)), pltpu.SemaphoreType.DMA((8,)),
            pltpu.SemaphoreType.DMA((4,)), pltpu.SemaphoreType.DMA((4,)),
            pltpu.SemaphoreType.DMA((4,)), pltpu.SemaphoreType.DMA((4,)),
            pltpu.SemaphoreType.DMA((8,)), pltpu.SemaphoreType.DMA((8,)),
            pltpu.SemaphoreType.DMA],
        compiler_params=pltpu.CompilerParams(collective_id=0, has_side_effects=True, vmem_limit_bytes=32 * 2**20),
    )(agg.reshape(J, AGG, LANES), decay_rates)

    return pl.pallas_call(
        finish_kernel,
        name="finish",
        out_shape=sds((T, E), bf16),
        in_specs=[ANY, ANY, ANY, ANY, ANY, VMEM, VMEM, VMEM],
        out_specs=ANY,
        scratch_shapes=[
            pltpu.VMEM((G, ROWS, LANES), f32), pltpu.VMEM((G, ROWS, LANES), f32), pltpu.VMEM((G, T, GW), bf16),
            pltpu.VMEM((T * N, LANES), f32), pltpu.VMEM((G, T, GW), bf16),
            pltpu.VMEM((G, N * J, LANES), f32), pltpu.VMEM((N * J, LANES), f32), pltpu.VMEM((G, T, GW), bf16),
            pltpu.SemaphoreType.DMA((5, G)), pltpu.SemaphoreType.DMA((G,))],
        compiler_params=pltpu.CompilerParams(vmem_limit_bytes=VMEM_BYTES),
    )(y, c, u, cs, gate_in, carry.reshape(J * G * N, LANES), decay_rates, skip_gain.reshape(1, E))


def solution(mesh):
    tokens = P(("outer", "inner"), None)
    return jax.shard_map(
        local, mesh=mesh, in_specs=(tokens, tokens, P(), P(), P(), P(), P(), P(), P()),
        out_specs=tokens, check_vma=False)
```

```python
import math

import jax
import jax.numpy as jnp
from jax import lax
from jax.experimental import pallas as pl
from jax.experimental.pallas import tpu as pltpu
from jax.sharding import PartitionSpec as P

f32, bf16 = jnp.float32, jnp.bfloat16
MESH = pl.DeviceIdType.MESH
LOG2E = math.log2(math.e)
LN2 = math.log(2.0)
DT_CEILING = 0.25

T = 128
E = 8192
N = 16
R = 256
KW = 4
LANES = 128
J = 8
GW = J * LANES
G = E // GW
ROWS = T * J
C = G // 2
AGG = 40
HALO = 16


def silu(v):
    d = 1.0 + jnp.exp2(v * -LOG2E)
    r = pl.reciprocal(d, approx=True)
    r = r * (2.0 - d * r)
    return v * r


def softplus_clipped(v):
    z = jnp.exp2(jnp.minimum(v, 0.0) * LOG2E)
    small = z * (1.0 - z * (0.5 - z * (1.0 / 3.0 - 0.25 * z)))
    big = jnp.log2(1.0 + z) * LN2
    return jnp.minimum(jnp.where(z < 0.03, small, big), DT_CEILING)


def split3(v):
    hi = v.astype(bf16).astype(f32)
    mid = (v - hi).astype(bf16).astype(f32)
    lo = (v - hi - mid).astype(bf16).astype(f32)
    return hi, mid, lo


def kernel(x_hbm, gate_hbm, cw_hbm, cb_hbm, xp_hbm, dp_hbm, db_hbm, a_hbm, sk_hbm, out_hbm,
           x_v, gate_v, cw_v, cb_v, xp_v, dp_v, db_v, a_v, sk_v, halo_v, xch_v, wch_v, u_v, bs_v, cs_v, ach_v,
           proj_v, dch_v, ich_v, ych_v, cch_v, out_v,
           agg_v, got_v, total_v, ys_v, part_v, ytotal_v, zs_v, back_v, carry_v,
           in_sem, one_sem, out_sem, hsend, hrecv, send1, recv1, sendy, recvy, sendz, recvz, send4, recv4):
    outer, x = lax.axis_index("outer"), lax.axis_index("inner")
    core, y, z = outer % 2, (outer // 2) % 4, outer // 8
    me = core * 4 + x
    line = outer * 4 + x

    def in_copy(kind, g):
        cols = pl.ds(pl.multiple_of(g * GW, GW), GW)
        source, target = ((x_hbm, x_v), (xp_hbm, xp_v), (dp_hbm, dp_v), (gate_hbm, gate_v))[kind]
        return pltpu.make_async_copy(source.at[:, cols], target.at[g], in_sem.at[kind, g])

    ones = [pltpu.make_async_copy(s, t, one_sem.at[k]) for k, (s, t) in enumerate(
        ((cw_hbm, cw_v), (cb_hbm, cb_v), (a_hbm, a_v), (db_hbm, db_v), (sk_hbm, sk_v)))]
    for cp in ones[:2]:
        cp.start()
    for g in range(G):
        in_copy(0, g).start()
        in_copy(1, g).start()
    for cp in ones[2:]:
        cp.start()
    for g in range(G):
        in_copy(2, g).start()
    for g in range(G):
        in_copy(3, g).start()

    def at_line(v):
        return (v // 4, v % 4)

    def member(m):
        return ((z * 4 + y) * 2 + m // 4, m % 4)

    def at_y(v):
        return ((z * 4 + v) * 2 + core, x)

    def at_z(v):
        return ((v * 4 + y) * 2 + core, x)

    devices = lax.axis_size("outer") * lax.axis_size("inner")
    barrier = pltpu.get_barrier_semaphore()
    after, before = (line + 1) % devices, (line + devices - 1) % devices
    pl.semaphore_signal(barrier, inc=1, device_id=at_line(after), device_id_type=MESH)
    pl.semaphore_signal(barrier, inc=1, device_id=at_line(before), device_id_type=MESH)
    for r in range(1, 8):
        pl.semaphore_signal(barrier, inc=1, device_id=member((me + r) % 8), device_id_type=MESH)
    for r in range(1, 4):
        pl.semaphore_signal(barrier, inc=1, device_id=at_y((y + r) % 4), device_id_type=MESH)
        pl.semaphore_signal(barrier, inc=1, device_id=at_z((z + r) % 4), device_id_type=MESH)
    pl.semaphore_wait(barrier, 15)

    def halo_copy(g):
        cols = pl.ds(pl.multiple_of(g * GW, GW), GW)
        return pltpu.make_async_remote_copy(
            src_ref=x_hbm.at[pl.ds(T - HALO, HALO), cols], dst_ref=halo_v.at[g], send_sem=hsend.at[g],
            recv_sem=hrecv.at[g], device_id=at_line(after), device_id_type=MESH)

    for g in range(G):
        halo_copy(g).start()

    def rows(index, count):
        return pl.ds(pl.multiple_of(index * count, 8), count)

    def first_copy(c, r):
        to = (me + r) % 8
        return pltpu.make_async_remote_copy(
            src_ref=agg_v.at[rows(c * 8 + to, AGG), :], dst_ref=got_v.at[rows(c * 8 + me, AGG), :],
            send_sem=send1.at[c, r], recv_sem=recv1.at[c, r], device_id=member(to), device_id_type=MESH)

    def y_copy(c, r):
        return pltpu.make_async_remote_copy(
            src_ref=total_v.at[rows(c, AGG), :], dst_ref=ys_v.at[rows(c * 4 + y, AGG), :],
            send_sem=sendy.at[c, r], recv_sem=recvy.at[c, r], device_id=at_y((y + r) % 4), device_id_type=MESH)

    def z_copy(c, r):
        return pltpu.make_async_remote_copy(
            src_ref=ytotal_v.at[rows(c, AGG), :], dst_ref=zs_v.at[rows(c * 4 + z, AGG), :],
            send_sem=sendz.at[c, r], recv_sem=recvz.at[c, r], device_id=at_z((z + r) % 4), device_id_type=MESH)

    def last_copy(c, r):
        to = (me + r) % 8
        return pltpu.make_async_remote_copy(
            src_ref=back_v.at[rows(c * 8 + to, 2 * N), :], dst_ref=carry_v.at[rows(c * 8 + me, 2 * N), :],
            send_sem=send4.at[c, r], recv_sem=recv4.at[c, r], device_id=member(to), device_id_type=MESH)

    agg_v[...] = jnp.zeros_like(agg_v)
    total_v[...] = jnp.zeros_like(total_v)
    ytotal_v[...] = jnp.zeros_like(ytotal_v)
    proj_v[...] = jnp.zeros_like(proj_v)
    for cp in ones[:2]:
        cp.wait()
    for q in range(E // LANES):
        g, j, cols = q // J, q % J, slice(q * LANES, (q + 1) * LANES)
        wch_v[g, pl.ds(j, KW, stride=J), :] = cw_v[:, cols]
        wch_v[g, KW * J + j:KW * J + j + 1, :] = cb_v[:, cols]

    def conv_group(g, _):
        in_copy(0, g).wait()
        halo_copy(g).wait_recv()
        for j in range(J):
            cols = slice(j * LANES, (j + 1) * LANES)
            halo = halo_v[g, :, cols].astype(f32)
            xch_v[pl.ds(j, HALO, stride=J), :] = jnp.where(line > 0, halo, 0.0)
            xch_v[pl.ds(HALO * J + j, T, stride=J), :] = x_v[g, :, cols].astype(f32)

        def tokens(k, _):
            w = [wch_v[g, i * J:(i + 1) * J, :] for i in range(KW + 1)]
            for tt in range(16):
                r = pl.multiple_of((k * 16 + tt) * J, J)
                acc = w[KW]
                for i in range(KW):
                    acc = acc + w[i] * xch_v[pl.ds(r + (HALO - KW + 1 + i) * J, J), :]
                dch_v[pl.ds(r, J), :] = silu(acc)
            return 0

        lax.fori_loop(0, T // 16, tokens, 0)
        for j in range(J):
            u_v[g, :, j * LANES:(j + 1) * LANES] = dch_v[pl.ds(j, T, stride=J), :].astype(bf16)
        in_copy(1, g).wait()
        proj_v[...] += lax.dot_general(u_v[g], xp_v[g], (((1,), (1,)), ((), ())), preferred_element_type=f32)
        return 0

    lax.fori_loop(0, G, conv_group, 0)

    row = lax.broadcasted_iota(jnp.int32, (256, 16), 0)
    col = lax.broadcasted_iota(jnp.int32, (256, 16), 1)
    repeat = (row // N == col).astype(bf16)
    row = lax.broadcasted_iota(jnp.int32, (256, 96), 0)
    col = lax.broadcasted_iota(jnp.int32, (256, 96), 1)
    own = row % N == col % N
    row = lax.broadcasted_iota(jnp.int32, (96, 256), 0)
    col = lax.broadcasted_iota(jnp.int32, (96, 256), 1)
    gather = (row // 48 == col // LANES).astype(bf16)

    def spread(k, _):
        r = pl.multiple_of(k * 16, 16)
        b = proj_v[pl.ds(r, 16), R:R + N]
        c = proj_v[pl.ds(r, 16), R + N:R + 2 * N]
        parts = jnp.concatenate([*split3(b), *split3(c)], axis=1).astype(bf16)
        wide = jnp.dot(repeat, parts, preferred_element_type=f32)
        wide = jnp.where(own, wide, 0.0).astype(bf16)
        full = jnp.dot(wide, gather, preferred_element_type=f32)
        r = pl.multiple_of(k * 256, 256)
        bs_v[pl.ds(r, 256), :] = full[:, :LANES]
        cs_v[pl.ds(r, 256), :] = full[:, LANES:]
        return 0

    lax.fori_loop(0, T // 16, spread, 0)

    for cp in ones[2:]:
        cp.wait()
    for q in range(E // LANES):
        ach_v[q // J, pl.ds(q % J, N, stride=J), :] = a_v[:, q * LANES:(q + 1) * LANES] * -LOG2E

    def scan_group(g, c, half):
        off = pl.multiple_of(g * GW, GW)
        in_copy(2, g).wait()
        dt_low = proj_v[:, 0:R].astype(bf16)
        for s in range(0, GW, 256):
            v = jnp.dot(dt_low, dp_v[g, :, s:s + 256], preferred_element_type=f32)
            d = softplus_clipped(v + db_v[:, pl.ds(off + s, 256)])
            i = d * u_v[g, :, s:s + 256].astype(f32)
            for h in range(2):
                j = s // LANES + h
                dch_v[pl.ds(j, T, stride=J), :] = d[:, h * LANES:(h + 1) * LANES]
                ich_v[pl.ds(j, T, stride=J), :] = i[:, h * LANES:(h + 1) * LANES]

        def steps(k, carry):
            h, cum = list(carry[0]), carry[1]
            for tt in range(UNROLL):
                t = k * UNROLL + tt
                r = pl.multiple_of(t * J, J)
                d = dch_v[pl.ds(r, J), :]
                i = ich_v[pl.ds(r, J), :]
                cum = cum + d
                cch_v[g, pl.ds(r, J), :] = cum
                ys = []
                for n in range(N):
                    e = jnp.exp2(d * ach_v[g, n * J:(n + 1) * J, :])
                    b = bs_v[pl.ds(t * N + n, J, stride=0), :]
                    c_n = cs_v[pl.ds(t * N + n, J, stride=0), :]
                    h[n] = e * h[n] + b * i
                    ys.append(c_n * h[n])
                    if n % 4 == 3:
                        y4 = (ys[0] + ys[1]) + (ys[2] + ys[3])
                        y_t = y4 if n == 3 else y_t + y4
                        ys = []
                ych_v[g, pl.ds(r, J), :] = y_t
            return tuple(h), cum

        zero = jnp.zeros((J, LANES), f32)
        h, cum = lax.fori_loop(0, T // UNROLL, steps, ((zero,) * N, zero))
        for n in range(N):
            agg_v[pl.ds(c * (J * AGG) + half * N + n, J, stride=AGG), :] = h[n]
        agg_v[pl.ds(c * (J * AGG) + 2 * N + half, J, stride=AGG), :] = cum

    def rates(c, half):
        col = pl.multiple_of((c * 2 + half) * GW + me * LANES, LANES)
        return a_v[:, pl.ds(col, LANES)] * -LOG2E

    def advance(state, ref, slot, rate, half):
        d = ref[pl.ds(slot * AGG + 2 * N + half, N, stride=0), :]
        return jnp.exp2(d * rate) * state + ref[pl.ds(pl.multiple_of(slot * AGG + half * N, 8), N), :]

    def dsums(ref, slot):
        return ref[pl.ds(pl.multiple_of(slot * AGG + 2 * N, 8), 8), :]

    def put(ref, slot, row, count, value):
        ref[pl.ds(pl.multiple_of(slot * AGG + row, 8), count), :] = value

    def send_first(c):
        got_v[rows(c * 8 + me, AGG), :] = agg_v[rows(c * 8 + me, AGG), :]
        for r in range(1, 8):
            first_copy(c, r).start()

    def after_first(c):
        for r in range(1, 8):
            first_copy(c, r).wait_recv()
        d = dsums(got_v, c * 8)
        for k in range(1, 8):
            d = d + dsums(got_v, c * 8 + k)
        put(total_v, c, 2 * N, 8, d)
        put(ys_v, c * 4 + y, 2 * N, 8, d)
        for half in range(2):
            rate = rates(c, half)
            s = jnp.zeros((N, LANES), f32)
            for k in range(8):
                s = advance(s, got_v, c * 8 + k, rate, half)
            put(total_v, c, half * N, N, s)
            put(ys_v, c * 4 + y, half * N, N, s)
        for r in range(1, 4):
            y_copy(c, r).start()

    def after_y(c):
        for r in range(1, 4):
            y_copy(c, r).wait_recv()
        d = dsums(ys_v, c * 4)
        pre = jnp.where(y > 0, d, 0.0)
        for k in range(1, 4):
            now = dsums(ys_v, c * 4 + k)
            d = d + now
            pre = pre + jnp.where(y > k, now, 0.0)
        put(part_v, c, 2 * N, 8, pre)
        put(ytotal_v, c, 2 * N, 8, d)
        put(zs_v, c * 4 + z, 2 * N, 8, d)
        for half in range(2):
            rate = rates(c, half)
            s = jnp.zeros((N, LANES), f32)
            pre = s
            for k in range(4):
                s = advance(s, ys_v, c * 4 + k, rate, half)
                pre = jnp.where(y > k, s, pre)
            put(part_v, c, half * N, N, pre)
            put(ytotal_v, c, half * N, N, s)
            put(zs_v, c * 4 + z, half * N, N, s)
        for r in range(1, 4):
            z_copy(c, r).start()

    def after_z(c):
        for r in range(1, 4):
            z_copy(c, r).wait_recv()
        for half in range(2):
            rate = rates(c, half)
            s = jnp.zeros((N, LANES), f32)
            pre = s
            for k in range(3):
                s = advance(s, zs_v, c * 4 + k, rate, half)
                pre = jnp.where(z > k, s, pre)
            s = advance(pre, part_v, c, rate, half)
            for k in range(8):
                back_v[pl.ds(pl.multiple_of((c * 8 + k) * 2 * N + half * N, 8), N), :] = s
                if k < 7:
                    s = advance(s, got_v, c * 8 + k, rate, half)
        carry_v[rows(c * 8 + me, 2 * N), :] = back_v[rows(c * 8 + me, 2 * N), :]
        for r in range(1, 8):
            last_copy(c, r).start()

    def first_half(p, _):
        scan_group(2 * p, p, 0)
        pl.when(p >= 1)(lambda: after_first(p - 1))
        pl.when(p >= 2)(lambda: after_y(p - 2))
        pl.when(p >= 3)(lambda: after_z(p - 3))
        scan_group(2 * p + 1, p, 1)
        send_first(p)
        return 0

    lax.fori_loop(0, C, first_half, 0)

    def out_copy(g):
        cols = pl.ds(pl.multiple_of(g * GW, GW), GW)
        return pltpu.make_async_copy(out_v.at[g], out_hbm.at[:, cols], out_sem.at[g])

    def finish_group(g, c, half):
        off = pl.multiple_of(g * GW, GW)

        def steps(k, _):
            for tt in range(UNROLL2):
                t = k * UNROLL2 + tt
                r = pl.multiple_of(t * J, J)
                cum = cch_v[g, pl.ds(r, J), :]
                y_t = ych_v[g, pl.ds(r, J), :]
                for n4 in range(0, N, 4):
                    part = []
                    for n in range(n4, n4 + 4):
                        e = jnp.exp2(cum * ach_v[g, n * J:(n + 1) * J, :])
                        c_n = cs_v[pl.ds(t * N + n, J, stride=0), :]
                        h_n = hch_v[n * J:(n + 1) * J, :]
                        part.append(c_n * (e * h_n))
                    y_t = y_t + ((part[0] + part[1]) + (part[2] + part[3]))
                ych_v[g, pl.ds(r, J), :] = y_t
            return 0

        hch_v = ich_v.at[pl.ds(0, N * J), :]
        for n in range(N):
            hch_v[n * J:(n + 1) * J, :] = carry_v[pl.ds(c * (J * 2 * N) + half * N + n, J, stride=2 * N), :]
        lax.fori_loop(0, T // UNROLL2, steps, 0)
        in_copy(3, g).wait()
        for j in range(J):
            cols = slice(j * LANES, (j + 1) * LANES)
            y_t = ych_v[g, pl.ds(j, T, stride=J), :]
            y_t = y_t + sk_v[:, pl.ds(off + j * LANES, LANES)] * u_v[g, :, cols].astype(f32)
            out_v[g, :, cols] = (y_t * silu(gate_v[g, :, cols].astype(f32))).astype(bf16)
        out_copy(g).start()

    def second_half(c, _):
        for r in range(1, 8):
            last_copy(c, r).wait_recv()
        finish_group(2 * c, c, 0)
        pl.when(c == 0)(lambda: after_first(C - 1))
        pl.when(c <= 1)(lambda: after_y(C - 2 + c))
        pl.when(c <= 2)(lambda: after_z(C - 3 + c))
        finish_group(2 * c + 1, c, 1)
        return 0

    lax.fori_loop(0, C, second_half, 0)

    for g in range(G):
        out_copy(g).wait()
        halo_copy(g).wait_send()
    for c in range(C):
        for r in range(1, 8):
            first_copy(c, r).wait_send()
            last_copy(c, r).wait_send()
        for r in range(1, 4):
            y_copy(c, r).wait_send()
            z_copy(c, r).wait_send()


ANY = pl.BlockSpec(memory_space=pl.ANY)
UNROLL, UNROLL2 = 8, 8


def local(x_in, gate_in, conv_weight, conv_bias, x_proj, dt_proj, dt_bias, decay_rates, skip_gain):
    vmem, dma = pltpu.VMEM, pltpu.SemaphoreType.DMA
    return pl.pallas_call(
        kernel,
        name="selective_scan",
        out_shape=jax.ShapeDtypeStruct((T, E), bf16),
        in_specs=[ANY] * 9,
        out_specs=ANY,
        scratch_shapes=[
            vmem((G, T, GW), bf16), vmem((G, T, GW), bf16), vmem((KW, E), f32), vmem((1, E), f32),
            vmem((G, R + 2 * N, GW), bf16), vmem((G, R, GW), bf16), vmem((1, E), f32), vmem((N, E), f32), vmem((1, E), f32),
            vmem((G, HALO, GW), bf16), vmem(((HALO + T) * J, LANES), f32), vmem((G, (KW + 1) * J, LANES), f32),
            vmem((G, T, GW), bf16), vmem((T * N, LANES), f32), vmem((T * N, LANES), f32), vmem((G, N * J, LANES), f32),
            vmem((T, R + 2 * N), f32), vmem((ROWS, LANES), f32), vmem((ROWS, LANES), f32),
            vmem((G, ROWS, LANES), f32), vmem((G, ROWS, LANES), f32), vmem((G, T, GW), bf16),
            vmem((C * 8 * AGG, LANES), f32), vmem((C * 8 * AGG, LANES), f32), vmem((C * AGG, LANES), f32),
            vmem((C * 4 * AGG, LANES), f32), vmem((C * AGG, LANES), f32), vmem((C * AGG, LANES), f32),
            vmem((C * 4 * AGG, LANES), f32), vmem((C * 8 * 2 * N, LANES), f32), vmem((C * 8 * 2 * N, LANES), f32),
            dma((4, G)), dma((5,)), dma((G,)), dma((G,)), dma((G,)),
            dma((C, 8)), dma((C, 8)), dma((C, 4)), dma((C, 4)), dma((C, 4)), dma((C, 4)), dma((C, 8)), dma((C, 8))],
        compiler_params=pltpu.CompilerParams(collective_id=0, has_side_effects=True, vmem_limit_bytes=52 * 2**20),
    )(x_in, gate_in, conv_weight, conv_bias.reshape(1, E), x_proj.T, dt_proj, dt_bias.reshape(1, E), decay_rates,
      skip_gain.reshape(1, E))


def solution(mesh):
    tokens = P(("outer", "inner"), None)
    return jax.shard_map(
        local, mesh=mesh, in_specs=(tokens, tokens, P(), P(), P(), P(), P(), P(), P()),
        out_specs=tokens, check_vma=False)
```

```python
import math

import jax
import jax.numpy as jnp
from jax import lax
from jax.experimental import pallas as pl
from jax.experimental.pallas import tpu as pltpu
from jax.sharding import PartitionSpec as P

f32, bf16 = jnp.float32, jnp.bfloat16
MESH = pl.DeviceIdType.MESH
LOG2E = math.log2(math.e)
LN2 = math.log(2.0)
DT_CEILING = 0.25

T = 128
E = 8192
N = 16
R = 256
KW = 4
LANES = 128
J = 8
GW = J * LANES
G = E // GW
ROWS = T * J
C = G // 2
AGG = 40
HALO = 16


def silu(v):
    d = 1.0 + jnp.exp2(v * -LOG2E)
    r = pl.reciprocal(d, approx=True)
    r = r * (2.0 - d * r)
    return v * r


def softplus_clipped(v):
    z = jnp.exp2(jnp.minimum(v, 0.0) * LOG2E)
    small = z * (1.0 - z * (0.5 - z * (1.0 / 3.0 - 0.25 * z)))
    big = jnp.log2(1.0 + z) * LN2
    return jnp.minimum(jnp.where(z < 0.03, small, big), DT_CEILING)


def split3(v):
    hi = v.astype(bf16).astype(f32)
    mid = (v - hi).astype(bf16).astype(f32)
    lo = (v - hi - mid).astype(bf16).astype(f32)
    return hi, mid, lo


def kernel(x_hbm, cw_hbm, cb_hbm, xp_hbm, dp_hbm, db_hbm, a_hbm, sk_hbm, out_hbm,
           x_v, cw_v, cb_v, xp_v, dp_v, db_v, a_v, sk_v, halo_v, xch_v, wch_v, u_v, bs_v, cs_v, ach_v,
           proj_v, dch_v, ich_v, ych_v, cch_v, out_v,
           agg_v, got_v, total_v, ys_v, part_v, ytotal_v, zs_v, back_v, carry_v,
           in_sem, one_sem, out_sem, hsend, hrecv, send1, recv1, sendy, recvy, sendz, recvz, send4, recv4):
    outer, x = lax.axis_index("outer"), lax.axis_index("inner")
    core, y, z = outer % 2, (outer // 2) % 4, outer // 8
    me = core * 4 + x
    line = outer * 4 + x

    def in_copy(kind, g):
        cols = pl.ds(pl.multiple_of(g * GW, GW), GW)
        source, target = ((x_hbm, x_v), (xp_hbm, xp_v), (dp_hbm, dp_v))[kind]
        return pltpu.make_async_copy(source.at[:, cols], target.at[g], in_sem.at[kind, g])

    ones = [pltpu.make_async_copy(s, t, one_sem.at[k]) for k, (s, t) in enumerate(
        ((cw_hbm, cw_v), (cb_hbm, cb_v), (a_hbm, a_v), (db_hbm, db_v), (sk_hbm, sk_v)))]
    for cp in ones[:2]:
        cp.start()
    for g in range(AHEAD):
        in_copy(0, g).start()
        in_copy(1, g).start()
    for cp in ones[2:]:
        cp.start()

    def at_line(v):
        return (v // 4, v % 4)

    def member(m):
        return ((z * 4 + y) * 2 + m // 4, m % 4)

    def at_y(v):
        return ((z * 4 + v) * 2 + core, x)

    def at_z(v):
        return ((v * 4 + y) * 2 + core, x)

    devices = lax.axis_size("outer") * lax.axis_size("inner")
    barrier = pltpu.get_barrier_semaphore()
    after, before = (line + 1) % devices, (line + devices - 1) % devices
    pl.semaphore_signal(barrier, inc=1, device_id=at_line(after), device_id_type=MESH)
    pl.semaphore_signal(barrier, inc=1, device_id=at_line(before), device_id_type=MESH)
    for r in range(1, 8):
        pl.semaphore_signal(barrier, inc=1, device_id=member((me + r) % 8), device_id_type=MESH)
    for r in range(1, 4):
        pl.semaphore_signal(barrier, inc=1, device_id=at_y((y + r) % 4), device_id_type=MESH)
        pl.semaphore_signal(barrier, inc=1, device_id=at_z((z + r) % 4), device_id_type=MESH)
    pl.semaphore_wait(barrier, 15)

    def halo_copy(g):
        cols = pl.ds(pl.multiple_of(g * GW, GW), GW)
        return pltpu.make_async_remote_copy(
            src_ref=x_hbm.at[pl.ds(T - HALO, HALO), cols], dst_ref=halo_v.at[g], send_sem=hsend.at[g],
            recv_sem=hrecv.at[g], device_id=at_line(after), device_id_type=MESH)

    for g in range(G):
        halo_copy(g).start()

    def rows(index, count):
        return pl.ds(pl.multiple_of(index * count, 8), count)

    def first_copy(c, r):
        to = (me + r) % 8
        return pltpu.make_async_remote_copy(
            src_ref=agg_v.at[rows(c * 8 + to, AGG), :], dst_ref=got_v.at[rows(c * 8 + me, AGG), :],
            send_sem=send1.at[c, r], recv_sem=recv1.at[c, r], device_id=member(to), device_id_type=MESH)

    def y_copy(c, r):
        return pltpu.make_async_remote_copy(
            src_ref=total_v.at[rows(c, AGG), :], dst_ref=ys_v.at[rows(c * 4 + y, AGG), :],
            send_sem=sendy.at[c, r], recv_sem=recvy.at[c, r], device_id=at_y((y + r) % 4), device_id_type=MESH)

    def z_copy(c, r):
        return pltpu.make_async_remote_copy(
            src_ref=ytotal_v.at[rows(c, AGG), :], dst_ref=zs_v.at[rows(c * 4 + z, AGG), :],
            send_sem=sendz.at[c, r], recv_sem=recvz.at[c, r], device_id=at_z((z + r) % 4), device_id_type=MESH)

    def last_copy(c, r):
        to = (me + r) % 8
        return pltpu.make_async_remote_copy(
            src_ref=back_v.at[rows(c * 8 + to, 2 * N), :], dst_ref=carry_v.at[rows(c * 8 + me, 2 * N), :],
            send_sem=send4.at[c, r], recv_sem=recv4.at[c, r], device_id=member(to), device_id_type=MESH)

    agg_v[...] = jnp.zeros_like(agg_v)
    total_v[...] = jnp.zeros_like(total_v)
    ytotal_v[...] = jnp.zeros_like(ytotal_v)
    proj_v[...] = jnp.zeros_like(proj_v)
    for cp in ones[:2]:
        cp.wait()
    for q in range(E // LANES):
        g, j, cols = q // J, q % J, slice(q * LANES, (q + 1) * LANES)
        wch_v[g, pl.ds(j, KW, stride=J), :] = cw_v[:, cols]
        wch_v[g, KW * J + j:KW * J + j + 1, :] = cb_v[:, cols]

    def conv_group(g, _):
        @pl.when(g + AHEAD < G)
        def _():
            in_copy(0, g + AHEAD).start()
            in_copy(1, g + AHEAD).start()

        in_copy(2, g).start()
        in_copy(0, g).wait()
        halo_copy(g).wait_recv()
        for j in range(J):
            cols = slice(j * LANES, (j + 1) * LANES)
            halo = halo_v[g, :, cols].astype(f32)
            xch_v[pl.ds(j, HALO, stride=J), :] = jnp.where(line > 0, halo, 0.0)
            xch_v[pl.ds(HALO * J + j, T, stride=J), :] = x_v[g, :, cols].astype(f32)

        def tokens(k, _):
            w = [wch_v[g, i * J:(i + 1) * J, :] for i in range(KW + 1)]
            for tt in range(16):
                r = pl.multiple_of((k * 16 + tt) * J, J)
                acc = w[KW]
                for i in range(KW):
                    acc = acc + w[i] * xch_v[pl.ds(r + (HALO - KW + 1 + i) * J, J), :]
                dch_v[0, pl.ds(r, J), :] = silu(acc)
            return 0

        lax.fori_loop(0, T // 16, tokens, 0)
        for j in range(J):
            u_v[g, :, j * LANES:(j + 1) * LANES] = dch_v[0, pl.ds(j, T, stride=J), :].astype(bf16)
        in_copy(1, g).wait()
        proj_v[...] += lax.dot_general(u_v[g], xp_v[g], (((1,), (1,)), ((), ())), preferred_element_type=f32)
        return 0

    lax.fori_loop(0, G, conv_group, 0)

    row = lax.broadcasted_iota(jnp.int32, (256, 16), 0)
    col = lax.broadcasted_iota(jnp.int32, (256, 16), 1)
    repeat = (row // N == col).astype(bf16)
    row = lax.broadcasted_iota(jnp.int32, (256, 96), 0)
    col = lax.broadcasted_iota(jnp.int32, (256, 96), 1)
    own = row % N == col % N
    row = lax.broadcasted_iota(jnp.int32, (96, 256), 0)
    col = lax.broadcasted_iota(jnp.int32, (96, 256), 1)
    gather = (row // 48 == col // LANES).astype(bf16)

    def spread(k, _):
        r = pl.multiple_of(k * 16, 16)
        b = proj_v[pl.ds(r, 16), R:R + N]
        c = proj_v[pl.ds(r, 16), R + N:R + 2 * N]
        parts = jnp.concatenate([*split3(b), *split3(c)], axis=1).astype(bf16)
        wide = jnp.dot(repeat, parts, preferred_element_type=f32)
        wide = jnp.where(own, wide, 0.0).astype(bf16)
        full = jnp.dot(wide, gather, preferred_element_type=f32)
        r = pl.multiple_of(k * 256, 256)
        bs_v[pl.ds(r, 256), :] = full[:, :LANES]
        cs_v[pl.ds(r, 256), :] = full[:, LANES:]
        return 0

    lax.fori_loop(0, T // 16, spread, 0)

    for cp in ones[2:]:
        cp.wait()
    for q in range(E // LANES):
        ach_v[q // J, pl.ds(q % J, N, stride=J), :] = a_v[:, q * LANES:(q + 1) * LANES] * -LOG2E

    def steps_of(g, slot):
        off = pl.multiple_of(g * GW, GW)
        in_copy(2, g).wait()
        dt_low = proj_v[:, 0:R].astype(bf16)
        for s in range(0, GW, 256):
            v = jnp.dot(dt_low, dp_v[g, :, s:s + 256], preferred_element_type=f32)
            d = softplus_clipped(v + db_v[:, pl.ds(off + s, 256)])
            i = d * u_v[g, :, s:s + 256].astype(f32)
            for h in range(2):
                j = s // LANES + h
                dch_v[slot, pl.ds(j, T, stride=J), :] = d[:, h * LANES:(h + 1) * LANES]
                ich_v[slot, pl.ds(j, T, stride=J), :] = i[:, h * LANES:(h + 1) * LANES]

    def recur(g, slot, h, cum, unroll, emit):
        def steps(k, carry):
            h, cum = list(carry[0]), carry[1]
            for tt in range(unroll):
                t = k * unroll + tt
                r = pl.multiple_of(t * J, J)
                d = dch_v[slot, pl.ds(r, J), :]
                i = ich_v[slot, pl.ds(r, J), :]
                if cum is not None:
                    cum = cum + d
                ys = []
                for n in range(N):
                    e = jnp.exp2(d * ach_v[g, n * J:(n + 1) * J, :])
                    b = bs_v[pl.ds(t * N + n, J, stride=0), :]
                    h[n] = e * h[n] + b * i
                    if emit is not None:
                        ys.append(cs_v[pl.ds(t * N + n, J, stride=0), :] * h[n])
                        if n % 4 == 3:
                            y4 = (ys[0] + ys[1]) + (ys[2] + ys[3])
                            y_t = y4 if n == 3 else y_t + y4
                            ys = []
                if emit is not None:
                    emit(r, y_t, cum)
            return tuple(h), cum

        return lax.fori_loop(0, T // unroll, steps, (tuple(h), cum))

    zero = jnp.zeros((J, LANES), f32)

    def aggregate(c, half, h, cum):
        for n in range(N):
            agg_v[pl.ds(c * (J * AGG) + half * N + n, J, stride=AGG), :] = h[n]
        agg_v[pl.ds(c * (J * AGG) + 2 * N + half, J, stride=AGG), :] = cum

    def carried(c, half, n):
        return carry_v[pl.ds(c * (J * 2 * N) + half * N + n, J, stride=2 * N), :]

    def final_state(p, half):
        g = 2 * p + half
        steps_of(g, g)
        aggregate(p, half, *recur(g, g, (zero,) * N, zero, UNROLL_S, None))

    def from_zero(p, half):
        g = 2 * p + half
        steps_of(g, G // 2)

        def emit(r, y_t, cum):
            ych_v[g, pl.ds(r, J), :] = y_t
            cch_v[g - G // 2, pl.ds(r, J), :] = cum

        aggregate(p, half, *recur(g, G // 2, (zero,) * N, zero, UNROLL_L, emit))

    def rates(c, half):
        col = pl.multiple_of((c * 2 + half) * GW + me * LANES, LANES)
        return a_v[:, pl.ds(col, LANES)] * -LOG2E

    def advance(state, ref, slot, rate, half):
        d = ref[pl.ds(slot * AGG + 2 * N + half, N, stride=0), :]
        return jnp.exp2(d * rate) * state + ref[pl.ds(pl.multiple_of(slot * AGG + half * N, 8), N), :]

    def dsums(ref, slot):
        return ref[pl.ds(pl.multiple_of(slot * AGG + 2 * N, 8), 8), :]

    def put(ref, slot, row, count, value):
        ref[pl.ds(pl.multiple_of(slot * AGG + row, 8), count), :] = value

    def send_first(c):
        got_v[rows(c * 8 + me, AGG), :] = agg_v[rows(c * 8 + me, AGG), :]
        for r in range(1, 8):
            first_copy(c, r).start()

    def after_first(c):
        for r in range(1, 8):
            first_copy(c, r).wait_recv()
        d = dsums(got_v, c * 8)
        for k in range(1, 8):
            d = d + dsums(got_v, c * 8 + k)
        put(total_v, c, 2 * N, 8, d)
        put(ys_v, c * 4 + y, 2 * N, 8, d)
        for half in range(2):
            rate = rates(c, half)
            s = jnp.zeros((N, LANES), f32)
            for k in range(8):
                s = advance(s, got_v, c * 8 + k, rate, half)
            put(total_v, c, half * N, N, s)
            put(ys_v, c * 4 + y, half * N, N, s)
        for r in range(1, 4):
            y_copy(c, r).start()

    def after_y(c):
        for r in range(1, 4):
            y_copy(c, r).wait_recv()
        d = dsums(ys_v, c * 4)
        pre = jnp.where(y > 0, d, 0.0)
        for k in range(1, 4):
            now = dsums(ys_v, c * 4 + k)
            d = d + now
            pre = pre + jnp.where(y > k, now, 0.0)
        put(part_v, c, 2 * N, 8, pre)
        put(ytotal_v, c, 2 * N, 8, d)
        put(zs_v, c * 4 + z, 2 * N, 8, d)
        for half in range(2):
            rate = rates(c, half)
            s = jnp.zeros((N, LANES), f32)
            pre = s
            for k in range(4):
                s = advance(s, ys_v, c * 4 + k, rate, half)
                pre = jnp.where(y > k, s, pre)
            put(part_v, c, half * N, N, pre)
            put(ytotal_v, c, half * N, N, s)
            put(zs_v, c * 4 + z, half * N, N, s)
        for r in range(1, 4):
            z_copy(c, r).start()

    def after_z(c):
        for r in range(1, 4):
            z_copy(c, r).wait_recv()
        for half in range(2):
            rate = rates(c, half)
            s = jnp.zeros((N, LANES), f32)
            pre = s
            for k in range(3):
                s = advance(s, zs_v, c * 4 + k, rate, half)
                pre = jnp.where(z > k, s, pre)
            s = advance(pre, part_v, c, rate, half)
            for k in range(8):
                back_v[pl.ds(pl.multiple_of((c * 8 + k) * 2 * N + half * N, 8), N), :] = s
                if k < 7:
                    s = advance(s, got_v, c * 8 + k, rate, half)
        carry_v[rows(c * 8 + me, 2 * N), :] = back_v[rows(c * 8 + me, 2 * N), :]
        for r in range(1, 8):
            last_copy(c, r).start()

    def out_copy(g):
        cols = pl.ds(pl.multiple_of(g * GW, GW), GW)
        return pltpu.make_async_copy(out_v.at[g], out_hbm.at[:, cols], out_sem.at[g])

    def finish(g):
        off = pl.multiple_of(g * GW, GW)
        for j in range(J):
            cols = slice(j * LANES, (j + 1) * LANES)
            y_t = ych_v[g, pl.ds(j, T, stride=J), :]
            out_v[g, :, cols] = y_t + sk_v[:, pl.ds(off + j * LANES, LANES)] * u_v[g, :, cols].astype(f32)
        out_copy(g).start()

    def wait_carry(c):
        for r in range(1, 8):
            last_copy(c, r).wait_recv()

    def from_carry(p, half):
        c = p - C
        g = 2 * c + half
        if half == 0:
            wait_carry(c)

        def emit(r, y_t, cum):
            ych_v[g, pl.ds(r, J), :] = y_t

        recur(g, g, [carried(c, half, n) for n in range(N)], None, UNROLL_F, emit)
        finish(g)

    def add_carry(p, half):
        c = p - C
        g = 2 * c + half
        if half == 0:
            wait_carry(c)
        hch_v = dch_v.at[0, pl.ds(0, N * J), :]
        for n in range(N):
            hch_v[n * J:(n + 1) * J, :] = carried(c, half, n)

        def steps(k, _):
            for tt in range(UNROLL_C):
                t = k * UNROLL_C + tt
                r = pl.multiple_of(t * J, J)
                cum = cch_v[g - G // 2, pl.ds(r, J), :]
                y_t = ych_v[g, pl.ds(r, J), :]
                for n4 in range(0, N, 4):
                    part = []
                    for n in range(n4, n4 + 4):
                        e = jnp.exp2(cum * ach_v[g, n * J:(n + 1) * J, :])
                        c_n = cs_v[pl.ds(t * N + n, J, stride=0), :]
                        part.append(c_n * (e * hch_v[n * J:(n + 1) * J, :]))
                    y_t = y_t + ((part[0] + part[1]) + (part[2] + part[3]))
                ych_v[g, pl.ds(r, J), :] = y_t
            return 0

        lax.fori_loop(0, T // UNROLL_C, steps, 0)
        finish(g)

    def pair(work, lo, hi):
        def body(p, _):
            work(p, 0)
            if hi > 2 and lo < C + 2:
                pl.when((p >= 2) & (p < C + 2))(lambda: after_y(p - 2))
            work(p, 1)
            if hi <= C:
                send_first(p)
            if hi > 1 and lo <= C:
                pl.when((p >= 1) & (p <= C))(lambda: after_first(p - 1))
            if hi > 2 and lo < C + 2:
                pl.when((p >= 2) & (p < C + 2))(lambda: after_z(p - 2))
            return 0

        lax.fori_loop(lo, hi, body, 0)

    pair(final_state, 0, C // 2)
    pair(from_zero, C // 2, C)
    pair(from_carry, C, C + C // 2)
    pair(add_carry, C + C // 2, 2 * C)

    for g in range(G):
        out_copy(g).wait()
        halo_copy(g).wait_send()
    for c in range(C):
        for r in range(1, 8):
            first_copy(c, r).wait_send()
            last_copy(c, r).wait_send()
        for r in range(1, 4):
            y_copy(c, r).wait_send()
            z_copy(c, r).wait_send()


HBM = pl.BlockSpec(memory_space=pltpu.HBM)
UNROLL_S, UNROLL_L, UNROLL_F, UNROLL_C = 16, 16, 16, 16
AHEAD = 3


def local(x_in, gate_in, conv_weight, conv_bias, x_proj, dt_proj, dt_bias, decay_rates, skip_gain):
    vmem, dma = pltpu.VMEM, pltpu.SemaphoreType.DMA
    y = pl.pallas_call(
        kernel,
        name="selective_scan",
        out_shape=jax.ShapeDtypeStruct((T, E), f32),
        in_specs=[HBM] * 8,
        out_specs=HBM,
        scratch_shapes=[
            vmem((G, T, GW), bf16), vmem((KW, E), f32), vmem((1, E), f32),
            vmem((G, R + 2 * N, GW), bf16), vmem((G, R, GW), bf16), vmem((1, E), f32), vmem((N, E), f32), vmem((1, E), f32),
            vmem((G, HALO, GW), bf16), vmem(((HALO + T) * J, LANES), f32), vmem((G, (KW + 1) * J, LANES), f32),
            vmem((G, T, GW), bf16), vmem((T * N, LANES), f32), vmem((T * N, LANES), f32), vmem((G, N * J, LANES), f32),
            vmem((T, R + 2 * N), f32), vmem((G // 2 + 1, ROWS, LANES), f32), vmem((G // 2 + 1, ROWS, LANES), f32),
            vmem((G, ROWS, LANES), f32), vmem((G // 2, ROWS, LANES), f32), vmem((G, T, GW), f32),
            vmem((C * 8 * AGG, LANES), f32), vmem((C * 8 * AGG, LANES), f32), vmem((C * AGG, LANES), f32),
            vmem((C * 4 * AGG, LANES), f32), vmem((C * AGG, LANES), f32), vmem((C * AGG, LANES), f32),
            vmem((C * 4 * AGG, LANES), f32), vmem((C * 8 * 2 * N, LANES), f32), vmem((C * 8 * 2 * N, LANES), f32),
            dma((3, G)), dma((5,)), dma((G,)), dma((G,)), dma((G,)),
            dma((C, 8)), dma((C, 8)), dma((C, 4)), dma((C, 4)), dma((C, 4)), dma((C, 4)), dma((C, 8)), dma((C, 8))],
        compiler_params=pltpu.CompilerParams(collective_id=0, has_side_effects=True, vmem_limit_bytes=60 * 2**20),
    )(x_in, conv_weight, conv_bias.reshape(1, E), x_proj.T, dt_proj, dt_bias.reshape(1, E), decay_rates,
      skip_gain.reshape(1, E))
    return (y * jax.nn.silu(gate_in.astype(f32))).astype(bf16)


def solution(mesh):
    tokens = P(("outer", "inner"), None)
    return jax.shard_map(
        local, mesh=mesh, in_specs=(tokens, tokens, P(), P(), P(), P(), P(), P(), P()),
        out_specs=tokens, check_vma=False)
```

```python
import math

import jax
import jax.numpy as jnp
from jax import lax
from jax.experimental import pallas as pl
from jax.experimental.pallas import tpu as pltpu
from jax.sharding import PartitionSpec as P

f32, bf16 = jnp.float32, jnp.bfloat16
MESH = pl.DeviceIdType.MESH
LOG2E = math.log2(math.e)
LN2 = math.log(2.0)
DT_CEILING = 0.25

T = 128
E = 8192
N = 16
R = 256
KW = 4
LANES = 128
J = 8
GW = J * LANES
G = E // GW
ROWS = T * J
C = G // 2
AGG = 40
HALO = 16


def silu(v):
    d = 1.0 + jnp.exp2(v * -LOG2E)
    r = pl.reciprocal(d, approx=True)
    r = r * (2.0 - d * r)
    return v * r


def softplus_clipped(v):
    z = jnp.exp2(jnp.minimum(v, 0.0) * LOG2E)
    small = z * (1.0 - z * (0.5 - z * (1.0 / 3.0 - 0.25 * z)))
    big = jnp.log2(1.0 + z) * LN2
    return jnp.minimum(jnp.where(z < 0.03, small, big), DT_CEILING)


def split3(v):
    hi = v.astype(bf16).astype(f32)
    mid = (v - hi).astype(bf16).astype(f32)
    lo = (v - hi - mid).astype(bf16).astype(f32)
    return hi, mid, lo


def kernel(x_hbm, cw_hbm, cb_hbm, xp_hbm, dp_hbm, db_hbm, a_hbm, sk_hbm, out_hbm,
           x_v, cw_v, cb_v, xp_v, dp_v, db_v, a_v, sk_v, halo_v, xch_v, wch_v, u_v, bs_v, cs_v, ach_v,
           proj_v, dch_v, ich_v, ych_v, cch_v, out_v,
           agg_v, got_v, total_v, ys_v, part_v, ytotal_v, zs_v, back_v, carry_v,
           in_sem, one_sem, out_sem, hsend, hrecv, send1, recv1, sendy, recvy, sendz, recvz, send4, recv4):
    outer, x = lax.axis_index("outer"), lax.axis_index("inner")
    core, y, z = outer % 2, (outer // 2) % 4, outer // 8
    me = core * 4 + x
    line = outer * 4 + x

    def in_copy(kind, g):
        cols = pl.ds(pl.multiple_of(g * GW, GW), GW)
        source, target = ((x_hbm, x_v), (xp_hbm, xp_v), (dp_hbm, dp_v))[kind]
        return pltpu.make_async_copy(source.at[:, cols], target.at[g], in_sem.at[kind, g])

    ones = [pltpu.make_async_copy(s, t, one_sem.at[k]) for k, (s, t) in enumerate(
        ((cw_hbm, cw_v), (cb_hbm, cb_v), (a_hbm, a_v), (db_hbm, db_v), (sk_hbm, sk_v)))]
    for cp in ones[:2]:
        cp.start()
    for g in range(G):
        in_copy(0, g).start()
    for cp in ones[2:]:
        cp.start()
    for g in range(AHEAD):
        in_copy(1, g).start()

    def at_line(v):
        return (v // 4, v % 4)

    def member(m):
        return ((z * 4 + y) * 2 + m // 4, m % 4)

    def at_y(v):
        return ((z * 4 + v) * 2 + core, x)

    def at_z(v):
        return ((v * 4 + y) * 2 + core, x)

    devices = lax.axis_size("outer") * lax.axis_size("inner")
    barrier = pltpu.get_barrier_semaphore()
    after, before = (line + 1) % devices, (line + devices - 1) % devices
    pl.semaphore_signal(barrier, inc=1, device_id=at_line(after), device_id_type=MESH)
    pl.semaphore_signal(barrier, inc=1, device_id=at_line(before), device_id_type=MESH)
    for r in range(1, 8):
        pl.semaphore_signal(barrier, inc=1, device_id=member((me + r) % 8), device_id_type=MESH)
    for r in range(1, 4):
        pl.semaphore_signal(barrier, inc=1, device_id=at_y((y + r) % 4), device_id_type=MESH)
        pl.semaphore_signal(barrier, inc=1, device_id=at_z((z + r) % 4), device_id_type=MESH)

    def halo_copy(g):
        cols = pl.ds(pl.multiple_of(g * GW, GW), GW)
        return pltpu.make_async_remote_copy(
            src_ref=x_hbm.at[pl.ds(T - HALO, HALO), cols], dst_ref=halo_v.at[g], send_sem=hsend.at[g],
            recv_sem=hrecv.at[g], device_id=at_line(after), device_id_type=MESH)

    def rows(index, count):
        return pl.ds(pl.multiple_of(index * count, 8), count)

    def first_copy(c, r):
        to = (me + r) % 8
        return pltpu.make_async_remote_copy(
            src_ref=agg_v.at[rows(c * 8 + to, AGG), :], dst_ref=got_v.at[rows(c * 8 + me, AGG), :],
            send_sem=send1.at[c, r], recv_sem=recv1.at[c, r], device_id=member(to), device_id_type=MESH)

    def y_copy(c, r):
        return pltpu.make_async_remote_copy(
            src_ref=total_v.at[rows(c, AGG), :], dst_ref=ys_v.at[rows(c * 4 + y, AGG), :],
            send_sem=sendy.at[c, r], recv_sem=recvy.at[c, r], device_id=at_y((y + r) % 4), device_id_type=MESH)

    def z_copy(c, r):
        return pltpu.make_async_remote_copy(
            src_ref=ytotal_v.at[rows(c, AGG), :], dst_ref=zs_v.at[rows(c * 4 + z, AGG), :],
            send_sem=sendz.at[c, r], recv_sem=recvz.at[c, r], device_id=at_z((z + r) % 4), device_id_type=MESH)

    def last_copy(c, r):
        to = (me + r) % 8
        return pltpu.make_async_remote_copy(
            src_ref=back_v.at[rows(c * 8 + to, 2 * N), :], dst_ref=carry_v.at[rows(c * 8 + me, 2 * N), :],
            send_sem=send4.at[c, r], recv_sem=recv4.at[c, r], device_id=member(to), device_id_type=MESH)

    agg_v[...] = jnp.zeros_like(agg_v)
    total_v[...] = jnp.zeros_like(total_v)
    ytotal_v[...] = jnp.zeros_like(ytotal_v)
    proj_v[...] = jnp.zeros_like(proj_v)
    for cp in ones[:2]:
        cp.wait()
    for q in range(E // LANES):
        g, j, cols = q // J, q % J, slice(q * LANES, (q + 1) * LANES)
        wch_v[g, pl.ds(j, KW, stride=J), :] = cw_v[:, cols]
        wch_v[g, KW * J + j:KW * J + j + 1, :] = cb_v[:, cols]

    def conv_tokens(g, k):
        w = [wch_v[g, i * J:(i + 1) * J, :] for i in range(KW + 1)]
        for tt in range(16):
            r = pl.multiple_of((k * 16 + tt) * J, J)
            acc = w[KW]
            for i in range(KW):
                acc = acc + w[i] * xch_v[g, pl.ds(r + (HALO - KW + 1 + i) * J, J), :]
            dch_v[0, pl.ds(r, J), :] = silu(acc)

    def conv_later(g):
        @pl.when(g + AHEAD < G)
        def _():
            in_copy(1, g + AHEAD).start()

        in_copy(0, g).wait()
        for j in range(J):
            xch_v[g, pl.ds(HALO * J + j, T, stride=J), :] = x_v[g, :, j * LANES:(j + 1) * LANES].astype(f32)

        def tokens(k, _):
            conv_tokens(g, k)
            return 0

        lax.fori_loop(1, T // 16, tokens, 0)
        for j in range(J):
            late = dch_v[0, pl.ds(16 * J + j, T - 16, stride=J), :]
            u_v[g, 16:T, j * LANES:(j + 1) * LANES] = late.astype(bf16)

    def conv_first(g, _):
        in_copy(2, g).start()
        halo_copy(g).wait_recv()
        for j in range(J):
            halo = halo_v[g, :, j * LANES:(j + 1) * LANES].astype(f32)
            xch_v[g, pl.ds(j, HALO, stride=J), :] = jnp.where(line > 0, halo, 0.0)
        conv_tokens(g, 0)
        for j in range(J):
            u_v[g, 0:16, j * LANES:(j + 1) * LANES] = dch_v[0, pl.ds(j, 16, stride=J), :].astype(bf16)
        in_copy(1, g).wait()
        proj_v[...] += lax.dot_general(u_v[g], xp_v[g], (((1,), (1,)), ((), ())), preferred_element_type=f32)
        return 0

    conv_later(0)
    pl.semaphore_wait(barrier, 15)
    for g in range(G):
        halo_copy(g).start()

    def rest(g, _):
        conv_later(g)
        return 0

    lax.fori_loop(1, G, rest, 0)
    for cp in ones[2:]:
        cp.wait()
    for q in range(E // LANES):
        ach_v[q // J, pl.ds(q % J, N, stride=J), :] = a_v[:, q * LANES:(q + 1) * LANES] * -LOG2E
    lax.fori_loop(0, G, conv_first, 0)

    row = lax.broadcasted_iota(jnp.int32, (256, 16), 0)
    col = lax.broadcasted_iota(jnp.int32, (256, 16), 1)
    repeat = (row // N == col).astype(bf16)
    row = lax.broadcasted_iota(jnp.int32, (256, 96), 0)
    col = lax.broadcasted_iota(jnp.int32, (256, 96), 1)
    own = row % N == col % N
    row = lax.broadcasted_iota(jnp.int32, (96, 256), 0)
    col = lax.broadcasted_iota(jnp.int32, (96, 256), 1)
    gather = (row // 48 == col // LANES).astype(bf16)

    def spread(k, _):
        r = pl.multiple_of(k * 16, 16)
        b = proj_v[pl.ds(r, 16), R:R + N]
        c = proj_v[pl.ds(r, 16), R + N:R + 2 * N]
        parts = jnp.concatenate([*split3(b), *split3(c)], axis=1).astype(bf16)
        wide = jnp.dot(repeat, parts, preferred_element_type=f32)
        wide = jnp.where(own, wide, 0.0).astype(bf16)
        full = jnp.dot(wide, gather, preferred_element_type=f32)
        r = pl.multiple_of(k * 256, 256)
        bs_v[pl.ds(r, 256), :] = full[:, :LANES]
        cs_v[pl.ds(r, 256), :] = full[:, LANES:]
        return 0

    lax.fori_loop(0, T // 16, spread, 0)

    def steps_of(g, slot):
        off = pl.multiple_of(g * GW, GW)
        in_copy(2, g).wait()
        dt_low = proj_v[:, 0:R].astype(bf16)
        for s in range(0, GW, 256):
            v = jnp.dot(dt_low, dp_v[g, :, s:s + 256], preferred_element_type=f32)
            d = softplus_clipped(v + db_v[:, pl.ds(off + s, 256)])
            i = d * u_v[g, :, s:s + 256].astype(f32)
            for h in range(2):
                j = s // LANES + h
                dch_v[slot, pl.ds(j, T, stride=J), :] = d[:, h * LANES:(h + 1) * LANES]
                ich_v[slot, pl.ds(j, T, stride=J), :] = i[:, h * LANES:(h + 1) * LANES]

    def recur(g, slot, h, cum, unroll, emit):
        def steps(k, carry):
            h, cum = list(carry[0]), carry[1]
            for tt in range(unroll):
                t = k * unroll + tt
                r = pl.multiple_of(t * J, J)
                d = dch_v[slot, pl.ds(r, J), :]
                i = ich_v[slot, pl.ds(r, J), :]
                if cum is not None:
                    cum = cum + d
                ys = []
                for n in range(N):
                    e = jnp.exp2(d * ach_v[g, n * J:(n + 1) * J, :])
                    b = bs_v[pl.ds(t * N + n, J, stride=0), :]
                    h[n] = e * h[n] + b * i
                    if emit is not None:
                        ys.append(cs_v[pl.ds(t * N + n, J, stride=0), :] * h[n])
                        if n % 4 == 3:
                            y4 = (ys[0] + ys[1]) + (ys[2] + ys[3])
                            y_t = y4 if n == 3 else y_t + y4
                            ys = []
                if emit is not None:
                    emit(r, y_t, cum)
            return tuple(h), cum

        return lax.fori_loop(0, T // unroll, steps, (tuple(h), cum))

    zero = jnp.zeros((J, LANES), f32)

    def aggregate(c, half, h, cum):
        for n in range(N):
            agg_v[pl.ds(c * (J * AGG) + half * N + n, J, stride=AGG), :] = h[n]
        agg_v[pl.ds(c * (J * AGG) + 2 * N + half, J, stride=AGG), :] = cum

    def carried(c, half, n):
        return carry_v[pl.ds(c * (J * 2 * N) + half * N + n, J, stride=2 * N), :]

    def final_state(p, half):
        g = 2 * p + half
        steps_of(g, g)
        aggregate(p, half, *recur(g, g, (zero,) * N, zero, UNROLL_S, None))

    def from_zero(p, half):
        g = 2 * p + half
        steps_of(g, G // 2)

        def emit(r, y_t, cum):
            ych_v[g, pl.ds(r, J), :] = y_t
            cch_v[g - G // 2, pl.ds(r, J), :] = cum

        aggregate(p, half, *recur(g, G // 2, (zero,) * N, zero, UNROLL_L, emit))

    def rates(c, half):
        col = pl.multiple_of((c * 2 + half) * GW + me * LANES, LANES)
        return a_v[:, pl.ds(col, LANES)] * -LOG2E

    def advance(state, ref, slot, rate, half):
        d = ref[pl.ds(slot * AGG + 2 * N + half, N, stride=0), :]
        return jnp.exp2(d * rate) * state + ref[pl.ds(pl.multiple_of(slot * AGG + half * N, 8), N), :]

    def dsums(ref, slot):
        return ref[pl.ds(pl.multiple_of(slot * AGG + 2 * N, 8), 8), :]

    def put(ref, slot, row, count, value):
        ref[pl.ds(pl.multiple_of(slot * AGG + row, 8), count), :] = value

    def send_first(c):
        got_v[rows(c * 8 + me, AGG), :] = agg_v[rows(c * 8 + me, AGG), :]
        for r in range(1, 8):
            first_copy(c, r).start()

    def after_first(c):
        for r in range(1, 8):
            first_copy(c, r).wait_recv()
        d = dsums(got_v, c * 8)
        for k in range(1, 8):
            d = d + dsums(got_v, c * 8 + k)
        put(total_v, c, 2 * N, 8, d)
        put(ys_v, c * 4 + y, 2 * N, 8, d)
        for half in range(2):
            rate = rates(c, half)
            s = jnp.zeros((N, LANES), f32)
            for k in range(8):
                s = advance(s, got_v, c * 8 + k, rate, half)
            put(total_v, c, half * N, N, s)
            put(ys_v, c * 4 + y, half * N, N, s)
        for r in range(1, 4):
            y_copy(c, r).start()

    def after_y(c):
        for r in range(1, 4):
            y_copy(c, r).wait_recv()
        d = dsums(ys_v, c * 4)
        pre = jnp.where(y > 0, d, 0.0)
        for k in range(1, 4):
            now = dsums(ys_v, c * 4 + k)
            d = d + now
            pre = pre + jnp.where(y > k, now, 0.0)
        put(part_v, c, 2 * N, 8, pre)
        put(ytotal_v, c, 2 * N, 8, d)
        put(zs_v, c * 4 + z, 2 * N, 8, d)
        for half in range(2):
            rate = rates(c, half)
            s = jnp.zeros((N, LANES), f32)
            pre = s
            for k in range(4):
                s = advance(s, ys_v, c * 4 + k, rate, half)
                pre = jnp.where(y > k, s, pre)
            put(part_v, c, half * N, N, pre)
            put(ytotal_v, c, half * N, N, s)
            put(zs_v, c * 4 + z, half * N, N, s)
        for r in range(1, 4):
            z_copy(c, r).start()

    def after_z(c):
        for r in range(1, 4):
            z_copy(c, r).wait_recv()
        for half in range(2):
            rate = rates(c, half)
            s = jnp.zeros((N, LANES), f32)
            pre = s
            for k in range(3):
                s = advance(s, zs_v, c * 4 + k, rate, half)
                pre = jnp.where(z > k, s, pre)
            s = advance(pre, part_v, c, rate, half)
            for k in range(8):
                back_v[pl.ds(pl.multiple_of((c * 8 + k) * 2 * N + half * N, 8), N), :] = s
                if k < 7:
                    s = advance(s, got_v, c * 8 + k, rate, half)
        carry_v[rows(c * 8 + me, 2 * N), :] = back_v[rows(c * 8 + me, 2 * N), :]
        for r in range(1, 8):
            last_copy(c, r).start()

    def out_copy(g):
        cols = pl.ds(pl.multiple_of(g * GW, GW), GW)
        return pltpu.make_async_copy(out_v.at[g], out_hbm.at[:, cols], out_sem.at[g])

    def finish(g):
        off = pl.multiple_of(g * GW, GW)
        for j in range(J):
            cols = slice(j * LANES, (j + 1) * LANES)
            y_t = ych_v[g, pl.ds(j, T, stride=J), :]
            out_v[g, :, cols] = y_t + sk_v[:, pl.ds(off + j * LANES, LANES)] * u_v[g, :, cols].astype(f32)
        out_copy(g).start()

    def wait_carry(c):
        for r in range(1, 8):
            last_copy(c, r).wait_recv()

    def from_carry(p, half):
        c = p - C
        g = 2 * c + half
        if half == 0:
            wait_carry(c)

        def emit(r, y_t, cum):
            ych_v[g, pl.ds(r, J), :] = y_t

        recur(g, g, [carried(c, half, n) for n in range(N)], None, UNROLL_F, emit)
        finish(g)

    def add_carry(p, half):
        c = p - C
        g = 2 * c + half
        if half == 0:
            wait_carry(c)
        hch_v = dch_v.at[0, pl.ds(0, N * J), :]
        for n in range(N):
            hch_v[n * J:(n + 1) * J, :] = carried(c, half, n)

        def steps(k, _):
            for tt in range(UNROLL_C):
                t = k * UNROLL_C + tt
                r = pl.multiple_of(t * J, J)
                cum = cch_v[g - G // 2, pl.ds(r, J), :]
                y_t = ych_v[g, pl.ds(r, J), :]
                for n4 in range(0, N, 4):
                    part = []
                    for n in range(n4, n4 + 4):
                        e = jnp.exp2(cum * ach_v[g, n * J:(n + 1) * J, :])
                        c_n = cs_v[pl.ds(t * N + n, J, stride=0), :]
                        part.append(c_n * (e * hch_v[n * J:(n + 1) * J, :]))
                    y_t = y_t + ((part[0] + part[1]) + (part[2] + part[3]))
                ych_v[g, pl.ds(r, J), :] = y_t
            return 0

        lax.fori_loop(0, T // UNROLL_C, steps, 0)
        finish(g)

    def pair(work, lo, hi):
        def body(p, _):
            work(p, 0)
            if hi > 2 and lo < C + 2:
                pl.when((p >= 2) & (p < C + 2))(lambda: after_y(p - 2))
            work(p, 1)
            if hi <= C:
                send_first(p)
            if hi > 1 and lo <= C:
                pl.when((p >= 1) & (p <= C))(lambda: after_first(p - 1))
            if hi > 2 and lo < C + 2:
                pl.when((p >= 2) & (p < C + 2))(lambda: after_z(p - 2))
            return 0

        lax.fori_loop(lo, hi, body, 0)

    pair(final_state, 0, C // 2)
    pair(from_zero, C // 2, C)
    pair(from_carry, C, C + C // 2)
    pair(add_carry, C + C // 2, 2 * C)

    for g in range(G):
        out_copy(g).wait()
        halo_copy(g).wait_send()
    for c in range(C):
        for r in range(1, 8):
            first_copy(c, r).wait_send()
            last_copy(c, r).wait_send()
        for r in range(1, 4):
            y_copy(c, r).wait_send()
            z_copy(c, r).wait_send()


HBM = pl.BlockSpec(memory_space=pltpu.HBM)
UNROLL_S, UNROLL_L, UNROLL_F, UNROLL_C = 16, 16, 16, 16
AHEAD = 3


def local(x_in, gate_in, conv_weight, conv_bias, x_proj, dt_proj, dt_bias, decay_rates, skip_gain):
    vmem, dma = pltpu.VMEM, pltpu.SemaphoreType.DMA
    y = pl.pallas_call(
        kernel,
        name="selective_scan",
        out_shape=jax.ShapeDtypeStruct((T, E), f32),
        in_specs=[HBM] * 8,
        out_specs=HBM,
        scratch_shapes=[
            vmem((G, T, GW), bf16), vmem((KW, E), f32), vmem((1, E), f32),
            vmem((G, R + 2 * N, GW), bf16), vmem((G, R, GW), bf16), vmem((1, E), f32), vmem((N, E), f32), vmem((1, E), f32),
            vmem((G, HALO, GW), bf16), vmem((G, (HALO + T) * J, LANES), f32), vmem((G, (KW + 1) * J, LANES), f32),
            vmem((G, T, GW), bf16), vmem((T * N, LANES), f32), vmem((T * N, LANES), f32), vmem((G, N * J, LANES), f32),
            vmem((T, R + 2 * N), f32), vmem((G // 2 + 1, ROWS, LANES), f32), vmem((G // 2 + 1, ROWS, LANES), f32),
            vmem((G, ROWS, LANES), f32), vmem((G // 2, ROWS, LANES), f32), vmem((G, T, GW), f32),
            vmem((C * 8 * AGG, LANES), f32), vmem((C * 8 * AGG, LANES), f32), vmem((C * AGG, LANES), f32),
            vmem((C * 4 * AGG, LANES), f32), vmem((C * AGG, LANES), f32), vmem((C * AGG, LANES), f32),
            vmem((C * 4 * AGG, LANES), f32), vmem((C * 8 * 2 * N, LANES), f32), vmem((C * 8 * 2 * N, LANES), f32),
            dma((3, G)), dma((5,)), dma((G,)), dma((G,)), dma((G,)),
            dma((C, 8)), dma((C, 8)), dma((C, 4)), dma((C, 4)), dma((C, 4)), dma((C, 4)), dma((C, 8)), dma((C, 8))],
        compiler_params=pltpu.CompilerParams(collective_id=0, has_side_effects=True, vmem_limit_bytes=60 * 2**20),
    )(x_in, conv_weight, conv_bias.reshape(1, E), x_proj.T, dt_proj, dt_bias.reshape(1, E), decay_rates,
      skip_gain.reshape(1, E))
    gate = gate_in.astype(f32)
    return (y * (gate * (0.5 * jnp.tanh(0.5 * gate) + 0.5))).astype(bf16)


def solution(mesh):
    tokens = P(("outer", "inner"), None)
    return jax.shard_map(
        local, mesh=mesh, in_specs=(tokens, tokens, P(), P(), P(), P(), P(), P(), P()),
        out_specs=tokens, check_vma=False)
```

```python
import math

import jax
import jax.numpy as jnp
from jax import lax
from jax.experimental import pallas as pl
from jax.experimental.pallas import tpu as pltpu
from jax.sharding import PartitionSpec as P

f32, bf16 = jnp.float32, jnp.bfloat16
MESH = pl.DeviceIdType.MESH
LOG2E = math.log2(math.e)
LN2 = math.log(2.0)
DT_CEILING = 0.25

T = 128
E = 8192
N = 16
R = 256
KW = 4
LANES = 128
J = 8
GW = J * LANES
G = E // GW
ROWS = T * J
C = G // 2
AGG = 40
HALO = 16


def silu(v):
    d = 1.0 + jnp.exp2(v * -LOG2E)
    r = pl.reciprocal(d, approx=True)
    r = r * (2.0 - d * r)
    return v * r


def softplus_clipped(v):
    z = jnp.exp2(jnp.minimum(v, 0.0) * LOG2E)
    small = z * (1.0 - z * (0.5 - z * (1.0 / 3.0 - 0.25 * z)))
    big = jnp.log2(1.0 + z) * LN2
    return jnp.minimum(jnp.where(z < 0.03, small, big), DT_CEILING)


def split3(v):
    hi = v.astype(bf16).astype(f32)
    mid = (v - hi).astype(bf16).astype(f32)
    lo = (v - hi - mid).astype(bf16).astype(f32)
    return hi, mid, lo


def kernel(x_hbm, cw_hbm, cb_hbm, xp_hbm, dp_hbm, db_hbm, a_hbm, sk_hbm, out_hbm,
           x_v, cw_v, cb_v, xp_v, dp_v, db_v, a_v, sk_v, halo_v, xch_v, wch_v, u_v, bs_v, cs_v, ach_v,
           proj_v, dch_v, ich_v, ych_v, cch_v, out_v,
           agg_v, got_v, total_v, ys_v, part_v, ytotal_v, zs_v, back_v, carry_v,
           in_sem, one_sem, out_sem, hsend, hrecv, send1, recv1, sendy, recvy, sendz, recvz, send4, recv4):
    outer, x = lax.axis_index("outer"), lax.axis_index("inner")
    core, y, z = outer % 2, (outer // 2) % 4, outer // 8
    me = core * 4 + x
    line = outer * 4 + x

    def in_copy(kind, g):
        cols = pl.ds(pl.multiple_of(g * GW, GW), GW)
        source, target = ((x_hbm, x_v), (xp_hbm, xp_v), (dp_hbm, dp_v))[kind]
        return pltpu.make_async_copy(source.at[:, cols], target.at[g], in_sem.at[kind, g])

    ones = [pltpu.make_async_copy(s, t, one_sem.at[k]) for k, (s, t) in enumerate(
        ((cw_hbm, cw_v), (cb_hbm, cb_v), (a_hbm, a_v), (db_hbm, db_v), (sk_hbm, sk_v)))]
    for cp in ones[:2]:
        cp.start()
    for g in range(G):
        in_copy(0, g).start()
    for cp in ones[2:]:
        cp.start()
    for g in range(AHEAD):
        in_copy(1, g).start()

    def at_line(v):
        return (v // 4, v % 4)

    def member(m):
        return ((z * 4 + y) * 2 + m // 4, m % 4)

    def at_y(v):
        return ((z * 4 + v) * 2 + core, x)

    def at_z(v):
        return ((v * 4 + y) * 2 + core, x)

    devices = lax.axis_size("outer") * lax.axis_size("inner")
    barrier = pltpu.get_barrier_semaphore()
    after, before = (line + 1) % devices, (line + devices - 1) % devices
    pl.semaphore_signal(barrier, inc=1, device_id=at_line(after), device_id_type=MESH)
    pl.semaphore_signal(barrier, inc=1, device_id=at_line(before), device_id_type=MESH)
    for r in range(1, 8):
        pl.semaphore_signal(barrier, inc=1, device_id=member((me + r) % 8), device_id_type=MESH)
    for r in range(1, 4):
        pl.semaphore_signal(barrier, inc=1, device_id=at_y((y + r) % 4), device_id_type=MESH)
        pl.semaphore_signal(barrier, inc=1, device_id=at_z((z + r) % 4), device_id_type=MESH)

    def halo_copy(g):
        cols = pl.ds(pl.multiple_of(g * GW, GW), GW)
        return pltpu.make_async_remote_copy(
            src_ref=x_hbm.at[pl.ds(T - HALO, HALO), cols], dst_ref=halo_v.at[g], send_sem=hsend.at[g],
            recv_sem=hrecv.at[g], device_id=at_line(after), device_id_type=MESH)

    def rows(index, count):
        return pl.ds(pl.multiple_of(index * count, 8), count)

    def first_copy(c, r):
        to = (me + r) % 8
        return pltpu.make_async_remote_copy(
            src_ref=agg_v.at[rows(c * 8 + to, AGG), :], dst_ref=got_v.at[rows(c * 8 + me, AGG), :],
            send_sem=send1.at[c, r], recv_sem=recv1.at[c, r], device_id=member(to), device_id_type=MESH)

    def y_copy(c, r):
        return pltpu.make_async_remote_copy(
            src_ref=total_v.at[rows(c, AGG), :], dst_ref=ys_v.at[rows(c * 4 + y, AGG), :],
            send_sem=sendy.at[c, r], recv_sem=recvy.at[c, r], device_id=at_y((y + r) % 4), device_id_type=MESH)

    def z_copy(c, r):
        return pltpu.make_async_remote_copy(
            src_ref=ytotal_v.at[rows(c, AGG), :], dst_ref=zs_v.at[rows(c * 4 + z, AGG), :],
            send_sem=sendz.at[c, r], recv_sem=recvz.at[c, r], device_id=at_z((z + r) % 4), device_id_type=MESH)

    def last_copy(c, r):
        to = (me + r) % 8
        return pltpu.make_async_remote_copy(
            src_ref=back_v.at[rows(c * 8 + to, 2 * N), :], dst_ref=carry_v.at[rows(c * 8 + me, 2 * N), :],
            send_sem=send4.at[c, r], recv_sem=recv4.at[c, r], device_id=member(to), device_id_type=MESH)

    agg_v[...] = jnp.zeros_like(agg_v)
    total_v[...] = jnp.zeros_like(total_v)
    ytotal_v[...] = jnp.zeros_like(ytotal_v)
    proj_v[...] = jnp.zeros_like(proj_v)
    for cp in ones[:2]:
        cp.wait()
    for q in range(E // LANES):
        g, j, cols = q // J, q % J, slice(q * LANES, (q + 1) * LANES)
        wch_v[g, pl.ds(j, KW, stride=J), :] = cw_v[:, cols]
        wch_v[g, KW * J + j:KW * J + j + 1, :] = cb_v[:, cols]

    def conv_tokens(g, k):
        w = [wch_v[g, i * J:(i + 1) * J, :] for i in range(KW + 1)]
        for tt in range(16):
            r = pl.multiple_of((k * 16 + tt) * J, J)
            acc = w[KW]
            for i in range(KW):
                acc = acc + w[i] * xch_v[g, pl.ds(r + (HALO - KW + 1 + i) * J, J), :]
            dch_v[0, pl.ds(r, J), :] = silu(acc)

    def conv_later(g):
        @pl.when(g + AHEAD < G)
        def _():
            in_copy(1, g + AHEAD).start()

        in_copy(0, g).wait()
        for j in range(J):
            xch_v[g, pl.ds(HALO * J + j, T, stride=J), :] = x_v[g, :, j * LANES:(j + 1) * LANES].astype(f32)

        def tokens(k, _):
            conv_tokens(g, k)
            return 0

        lax.fori_loop(1, T // 16, tokens, 0)
        for j in range(J):
            late = dch_v[0, pl.ds(16 * J + j, T - 16, stride=J), :]
            u_v[g, 16:T, j * LANES:(j + 1) * LANES] = late.astype(bf16)

    def conv_first(g, _):
        in_copy(2, g).start()
        halo_copy(g).wait_recv()
        for j in range(J):
            halo = halo_v[g, :, j * LANES:(j + 1) * LANES].astype(f32)
            xch_v[g, pl.ds(j, HALO, stride=J), :] = jnp.where(line > 0, halo, 0.0)
        conv_tokens(g, 0)
        for j in range(J):
            u_v[g, 0:16, j * LANES:(j + 1) * LANES] = dch_v[0, pl.ds(j, 16, stride=J), :].astype(bf16)
        in_copy(1, g).wait()
        proj_v[...] += lax.dot_general(u_v[g], xp_v[g], (((1,), (1,)), ((), ())), preferred_element_type=f32)
        return 0

    conv_later(0)
    pl.semaphore_wait(barrier, 15)
    for g in range(G):
        halo_copy(g).start()

    def rest(g, _):
        conv_later(g)
        return 0

    lax.fori_loop(1, G, rest, 0)
    for cp in ones[2:]:
        cp.wait()
    for q in range(E // LANES):
        ach_v[q // J, pl.ds(q % J, N, stride=J), :] = a_v[:, q * LANES:(q + 1) * LANES] * -LOG2E
    lax.fori_loop(0, G, conv_first, 0)

    row = lax.broadcasted_iota(jnp.int32, (256, 16), 0)
    col = lax.broadcasted_iota(jnp.int32, (256, 16), 1)
    repeat = (row // N == col).astype(bf16)
    row = lax.broadcasted_iota(jnp.int32, (256, 96), 0)
    col = lax.broadcasted_iota(jnp.int32, (256, 96), 1)
    own = row % N == col % N
    row = lax.broadcasted_iota(jnp.int32, (96, 256), 0)
    col = lax.broadcasted_iota(jnp.int32, (96, 256), 1)
    gather = (row // 48 == col // LANES).astype(bf16)

    def spread(k, _):
        r = pl.multiple_of(k * 16, 16)
        b = proj_v[pl.ds(r, 16), R:R + N]
        c = proj_v[pl.ds(r, 16), R + N:R + 2 * N]
        parts = jnp.concatenate([*split3(b), *split3(c)], axis=1).astype(bf16)
        wide = jnp.dot(repeat, parts, preferred_element_type=f32)
        wide = jnp.where(own, wide, 0.0).astype(bf16)
        full = jnp.dot(wide, gather, preferred_element_type=f32)
        r = pl.multiple_of(k * 256, 256)
        bs_v[pl.ds(r, 256), :] = full[:, :LANES]
        cs_v[pl.ds(r, 256), :] = full[:, LANES:]
        return 0

    lax.fori_loop(0, T // 16, spread, 0, unroll=True)

    def steps_of(g, slot):
        off = pl.multiple_of(g * GW, GW)
        in_copy(2, g).wait()
        dt_low = proj_v[:, 0:R].astype(bf16)
        for s in range(0, GW, 256):
            v = jnp.dot(dt_low, dp_v[g, :, s:s + 256], preferred_element_type=f32)
            d = softplus_clipped(v + db_v[:, pl.ds(off + s, 256)])
            i = d * u_v[g, :, s:s + 256].astype(f32)
            for h in range(2):
                j = s // LANES + h
                dch_v[slot, pl.ds(j, T, stride=J), :] = d[:, h * LANES:(h + 1) * LANES]
                ich_v[slot, pl.ds(j, T, stride=J), :] = i[:, h * LANES:(h + 1) * LANES]

    def recur(g, slot, h, cum, unroll, emit):
        def steps(k, carry):
            h, cum = list(carry[0]), carry[1]
            for tt in range(unroll):
                t = k * unroll + tt
                r = pl.multiple_of(t * J, J)
                d = dch_v[slot, pl.ds(r, J), :]
                i = ich_v[slot, pl.ds(r, J), :]
                if cum is not None:
                    cum = cum + d
                ys = []
                for n in range(N):
                    e = jnp.exp2(d * ach_v[g, n * J:(n + 1) * J, :])
                    b = bs_v[pl.ds(t * N + n, J, stride=0), :]
                    h[n] = e * h[n] + b * i
                    if emit is not None:
                        ys.append(cs_v[pl.ds(t * N + n, J, stride=0), :] * h[n])
                        if n % 4 == 3:
                            y4 = (ys[0] + ys[1]) + (ys[2] + ys[3])
                            y_t = y4 if n == 3 else y_t + y4
                            ys = []
                if emit is not None:
                    emit(r, y_t, cum)
            return tuple(h), cum

        return lax.fori_loop(0, T // unroll, steps, (tuple(h), cum))

    zero = jnp.zeros((J, LANES), f32)

    def aggregate(c, half, h, cum):
        for n in range(N):
            agg_v[pl.ds(c * (J * AGG) + half * N + n, J, stride=AGG), :] = h[n]
        agg_v[pl.ds(c * (J * AGG) + 2 * N + half, J, stride=AGG), :] = cum

    def carried(c, half, n):
        return carry_v[pl.ds(c * (J * 2 * N) + half * N + n, J, stride=2 * N), :]

    def final_state(p, half):
        g = 2 * p + half
        steps_of(g, g)
        aggregate(p, half, *recur(g, g, (zero,) * N, zero, UNROLL_S, None))

    def from_zero(p, half):
        g = 2 * p + half
        steps_of(g, G // 2)

        def emit(r, y_t, cum):
            ych_v[g, pl.ds(r, J), :] = y_t
            cch_v[g - G // 2, pl.ds(r, J), :] = cum

        aggregate(p, half, *recur(g, G // 2, (zero,) * N, zero, UNROLL_L, emit))

    def rates(c, half):
        col = pl.multiple_of((c * 2 + half) * GW + me * LANES, LANES)
        return a_v[:, pl.ds(col, LANES)] * -LOG2E

    def advance(state, ref, slot, rate, half):
        d = ref[pl.ds(slot * AGG + 2 * N + half, N, stride=0), :]
        return jnp.exp2(d * rate) * state + ref[pl.ds(pl.multiple_of(slot * AGG + half * N, 8), N), :]

    def dsums(ref, slot):
        return ref[pl.ds(pl.multiple_of(slot * AGG + 2 * N, 8), 8), :]

    def put(ref, slot, row, count, value):
        ref[pl.ds(pl.multiple_of(slot * AGG + row, 8), count), :] = value

    def send_first(c):
        got_v[rows(c * 8 + me, AGG), :] = agg_v[rows(c * 8 + me, AGG), :]
        for r in range(1, 8):
            first_copy(c, r).start()

    def after_first(c):
        for r in range(1, 8):
            first_copy(c, r).wait_recv()
        d = dsums(got_v, c * 8)
        for k in range(1, 8):
            d = d + dsums(got_v, c * 8 + k)
        put(total_v, c, 2 * N, 8, d)
        put(ys_v, c * 4 + y, 2 * N, 8, d)
        for half in range(2):
            rate = rates(c, half)
            s = jnp.zeros((N, LANES), f32)
            for k in range(8):
                s = advance(s, got_v, c * 8 + k, rate, half)
            put(total_v, c, half * N, N, s)
            put(ys_v, c * 4 + y, half * N, N, s)
        for r in range(1, 4):
            y_copy(c, r).start()

    def after_y(c):
        for r in range(1, 4):
            y_copy(c, r).wait_recv()
        d = dsums(ys_v, c * 4)
        pre = jnp.where(y > 0, d, 0.0)
        for k in range(1, 4):
            now = dsums(ys_v, c * 4 + k)
            d = d + now
            pre = pre + jnp.where(y > k, now, 0.0)
        put(part_v, c, 2 * N, 8, pre)
        put(ytotal_v, c, 2 * N, 8, d)
        put(zs_v, c * 4 + z, 2 * N, 8, d)
        for half in range(2):
            rate = rates(c, half)
            s = jnp.zeros((N, LANES), f32)
            pre = s
            for k in range(4):
                s = advance(s, ys_v, c * 4 + k, rate, half)
                pre = jnp.where(y > k, s, pre)
            put(part_v, c, half * N, N, pre)
            put(ytotal_v, c, half * N, N, s)
            put(zs_v, c * 4 + z, half * N, N, s)
        for r in range(1, 4):
            z_copy(c, r).start()

    def after_z(c):
        for r in range(1, 4):
            z_copy(c, r).wait_recv()
        for half in range(2):
            rate = rates(c, half)
            s = jnp.zeros((N, LANES), f32)
            pre = s
            for k in range(3):
                s = advance(s, zs_v, c * 4 + k, rate, half)
                pre = jnp.where(z > k, s, pre)
            s = advance(pre, part_v, c, rate, half)
            for k in range(8):
                back_v[pl.ds(pl.multiple_of((c * 8 + k) * 2 * N + half * N, 8), N), :] = s
                if k < 7:
                    s = advance(s, got_v, c * 8 + k, rate, half)
        carry_v[rows(c * 8 + me, 2 * N), :] = back_v[rows(c * 8 + me, 2 * N), :]
        for r in range(1, 8):
            last_copy(c, r).start()

    def out_copy(g):
        cols = pl.ds(pl.multiple_of(g * GW, GW), GW)
        return pltpu.make_async_copy(out_v.at[g], out_hbm.at[:, cols], out_sem.at[g])

    def finish(g):
        off = pl.multiple_of(g * GW, GW)
        for j in range(J):
            cols = slice(j * LANES, (j + 1) * LANES)
            y_t = ych_v[g, pl.ds(j, T, stride=J), :]
            out_v[g, :, cols] = y_t + sk_v[:, pl.ds(off + j * LANES, LANES)] * u_v[g, :, cols].astype(f32)
        out_copy(g).start()

    def wait_carry(c):
        for r in range(1, 8):
            last_copy(c, r).wait_recv()

    def from_carry(p, half):
        c = p - C
        g = 2 * c + half
        if half == 0:
            wait_carry(c)

        def emit(r, y_t, cum):
            ych_v[g, pl.ds(r, J), :] = y_t

        recur(g, g, [carried(c, half, n) for n in range(N)], None, UNROLL_F, emit)
        finish(g)

    def add_carry(p, half):
        c = p - C
        g = 2 * c + half
        if half == 0:
            wait_carry(c)
        hch_v = dch_v.at[0, pl.ds(0, N * J), :]
        for n in range(N):
            hch_v[n * J:(n + 1) * J, :] = carried(c, half, n)

        def steps(k, _):
            for tt in range(UNROLL_C):
                t = k * UNROLL_C + tt
                r = pl.multiple_of(t * J, J)
                cum = cch_v[g - G // 2, pl.ds(r, J), :]
                y_t = ych_v[g, pl.ds(r, J), :]
                for n4 in range(0, N, 4):
                    part = []
                    for n in range(n4, n4 + 4):
                        e = jnp.exp2(cum * ach_v[g, n * J:(n + 1) * J, :])
                        c_n = cs_v[pl.ds(t * N + n, J, stride=0), :]
                        part.append(c_n * (e * hch_v[n * J:(n + 1) * J, :]))
                    y_t = y_t + ((part[0] + part[1]) + (part[2] + part[3]))
                ych_v[g, pl.ds(r, J), :] = y_t
            return 0

        lax.fori_loop(0, T // UNROLL_C, steps, 0)
        finish(g)

    def pair(work, lo, hi):
        def body(p, _):
            work(p, 0)
            if hi > 2 and lo < C + 2:
                pl.when((p >= 2) & (p < C + 2))(lambda: after_y(p - 2))
            work(p, 1)
            if hi <= C:
                send_first(p)
            if hi > 1 and lo <= C:
                pl.when((p >= 1) & (p <= C))(lambda: after_first(p - 1))
            if hi > 2 and lo < C + 2:
                pl.when((p >= 2) & (p < C + 2))(lambda: after_z(p - 2))
            return 0

        lax.fori_loop(lo, hi, body, 0)

    pair(final_state, 0, C // 2)
    pair(from_zero, C // 2, C)
    pair(from_carry, C, C + C // 2)
    pair(add_carry, C + C // 2, 2 * C)

    for c in range(C):
        for r in range(1, 8):
            first_copy(c, r).wait_send()
            last_copy(c, r).wait_send()
        for r in range(1, 4):
            y_copy(c, r).wait_send()
            z_copy(c, r).wait_send()
    for g in range(G):
        halo_copy(g).wait_send()
        out_copy(g).wait()


ANY = pl.BlockSpec(memory_space=pl.ANY)
UNROLL_S, UNROLL_L, UNROLL_F, UNROLL_C = 16, 16, 16, 16
AHEAD = 3


def local(x_in, gate_in, conv_weight, conv_bias, x_proj, dt_proj, dt_bias, decay_rates, skip_gain):
    vmem, dma = pltpu.VMEM, pltpu.SemaphoreType.DMA
    y = pl.pallas_call(
        kernel,
        name="selective_scan",
        out_shape=pltpu.VMEM((T, E), f32),
        in_specs=[ANY] * 8,
        out_specs=ANY,
        scratch_shapes=[
            vmem((G, T, GW), bf16), vmem((KW, E), f32), vmem((1, E), f32),
            vmem((G, R + 2 * N, GW), bf16), vmem((G, R, GW), bf16), vmem((1, E), f32), vmem((N, E), f32), vmem((1, E), f32),
            vmem((G, HALO, GW), bf16), vmem((G, (HALO + T) * J, LANES), f32), vmem((G, (KW + 1) * J, LANES), f32),
            vmem((G, T, GW), bf16), vmem((T * N, LANES), f32), vmem((T * N, LANES), f32), vmem((G, N * J, LANES), f32),
            vmem((T, R + 2 * N), f32), vmem((G // 2 + 1, ROWS, LANES), f32), vmem((G // 2 + 1, ROWS, LANES), f32),
            vmem((G, ROWS, LANES), f32), vmem((G // 2, ROWS, LANES), f32), vmem((G, T, GW), f32),
            vmem((C * 8 * AGG, LANES), f32), vmem((C * 8 * AGG, LANES), f32), vmem((C * AGG, LANES), f32),
            vmem((C * 4 * AGG, LANES), f32), vmem((C * AGG, LANES), f32), vmem((C * AGG, LANES), f32),
            vmem((C * 4 * AGG, LANES), f32), vmem((C * 8 * 2 * N, LANES), f32), vmem((C * 8 * 2 * N, LANES), f32),
            dma((3, G)), dma((5,)), dma((G,)), dma((G,)), dma((G,)),
            dma((C, 8)), dma((C, 8)), dma((C, 4)), dma((C, 4)), dma((C, 4)), dma((C, 4)), dma((C, 8)), dma((C, 8))],
        compiler_params=pltpu.CompilerParams(collective_id=0, has_side_effects=True, vmem_limit_bytes=52 * 2**20),
    )(*(pltpu.with_memory_space_constraint(v, pltpu.HBM) for v in (
        x_in, conv_weight, conv_bias.reshape(1, E), x_proj.T, dt_proj, dt_bias.reshape(1, E), decay_rates,
        skip_gain.reshape(1, E))))
    gate = gate_in.astype(f32)
    return (y * (gate * (0.5 * jnp.tanh(0.5 * gate) + 0.5))).astype(bf16)


def solution(mesh):
    tokens = P(("outer", "inner"), None)
    return jax.shard_map(
        local, mesh=mesh, in_specs=(tokens, tokens, P(), P(), P(), P(), P(), P(), P()),
        out_specs=tokens, check_vma=False)
```

```python
import math

import jax
import jax.numpy as jnp
from jax import lax
from jax.experimental import pallas as pl
from jax.experimental.pallas import tpu as pltpu
from jax.sharding import PartitionSpec as P

f32, bf16 = jnp.float32, jnp.bfloat16
MESH = pl.DeviceIdType.MESH
LOG2E = math.log2(math.e)
LN2 = math.log(2.0)
DT_CEILING = 0.25

T = 128
E = 8192
N = 16
R = 256
KW = 4
LANES = 128
J = 8
GW = J * LANES
G = E // GW
ROWS = T * J
C = G // 2
AGG = 40
HALO = 16


def silu(v):
    d = 1.0 + jnp.exp2(v * -LOG2E)
    r = pl.reciprocal(d, approx=True)
    r = r * (2.0 - d * r)
    return v * r


def softplus_clipped(v):
    z = jnp.exp2(jnp.minimum(v, 0.0) * LOG2E)
    small = z * (1.0 - z * (0.5 - z * (1.0 / 3.0 - 0.25 * z)))
    big = jnp.log2(1.0 + z) * LN2
    return jnp.minimum(jnp.where(z < 0.03, small, big), DT_CEILING)


def split3(v):
    hi = v.astype(bf16).astype(f32)
    mid = (v - hi).astype(bf16).astype(f32)
    lo = (v - hi - mid).astype(bf16).astype(f32)
    return hi, mid, lo


def kernel(x_hbm, cw_hbm, cb_hbm, xp_hbm, dp_hbm, db_hbm, a_hbm, sk_hbm, out_hbm,
           x_v, cw_v, cb_v, xp_v, dp_v, db_v, a_v, sk_v, halo_v, xch_v, wch_v, u_v, bs_v, cs_v, ach_v,
           proj_v, dch_v, ich_v, ych_v, cch_v, out_v,
           agg_v, got_v, total_v, all_v, back_v, carry_v,
           in_sem, one_sem, out_sem, hsend, hrecv, send1, recv1, send2, recv2, send4, recv4):
    outer, x = lax.axis_index("outer"), lax.axis_index("inner")
    core, mine = outer % 2, outer // 2
    me = core * 4 + x
    line = outer * 4 + x

    def in_copy(kind, g):
        cols = pl.ds(pl.multiple_of(g * GW, GW), GW)
        source, target = ((x_hbm, x_v), (xp_hbm, xp_v), (dp_hbm, dp_v))[kind]
        return pltpu.make_async_copy(source.at[:, cols], target.at[g], in_sem.at[kind, g])

    ones = [pltpu.make_async_copy(s, t, one_sem.at[k]) for k, (s, t) in enumerate(
        ((cw_hbm, cw_v), (cb_hbm, cb_v), (a_hbm, a_v), (db_hbm, db_v), (sk_hbm, sk_v)))]
    for cp in ones[:2]:
        cp.start()
    for g in range(G):
        in_copy(0, g).start()
    for cp in ones[2:]:
        cp.start()
    for g in range(AHEAD):
        in_copy(1, g).start()

    def at_line(v):
        return (v // 4, v % 4)

    def member(m):
        return (mine * 2 + m // 4, m % 4)

    def peer(v):
        return (v * 2 + core, x)

    devices = lax.axis_size("outer") * lax.axis_size("inner")
    barrier = pltpu.get_barrier_semaphore()
    after, before = (line + 1) % devices, (line + devices - 1) % devices
    pl.semaphore_signal(barrier, inc=1, device_id=at_line(after), device_id_type=MESH)
    pl.semaphore_signal(barrier, inc=1, device_id=at_line(before), device_id_type=MESH)
    for r in range(1, 8):
        pl.semaphore_signal(barrier, inc=1, device_id=member((me + r) % 8), device_id_type=MESH)
    for r in range(1, 16):
        pl.semaphore_signal(barrier, inc=1, device_id=peer((mine + r) % 16), device_id_type=MESH)

    def halo_copy(g):
        cols = pl.ds(pl.multiple_of(g * GW, GW), GW)
        return pltpu.make_async_remote_copy(
            src_ref=x_hbm.at[pl.ds(T - HALO, HALO), cols], dst_ref=halo_v.at[g], send_sem=hsend.at[g],
            recv_sem=hrecv.at[g], device_id=at_line(after), device_id_type=MESH)

    def rows(index, count):
        return pl.ds(pl.multiple_of(index * count, 8), count)

    def first_copy(c, r):
        to = (me + r) % 8
        return pltpu.make_async_remote_copy(
            src_ref=agg_v.at[rows(c * 8 + to, AGG), :], dst_ref=got_v.at[rows(c * 8 + me, AGG), :],
            send_sem=send1.at[c, r], recv_sem=recv1.at[c, r], device_id=member(to), device_id_type=MESH)

    def group_copy(c, r):
        return pltpu.make_async_remote_copy(
            src_ref=total_v.at[rows(c, AGG), :], dst_ref=all_v.at[rows(c * 16 + mine, AGG), :],
            send_sem=send2.at[c, r], recv_sem=recv2.at[c, r], device_id=peer((mine + r) % 16), device_id_type=MESH)

    def last_copy(c, r):
        to = (me + r) % 8
        return pltpu.make_async_remote_copy(
            src_ref=back_v.at[rows(c * 8 + to, 2 * N), :], dst_ref=carry_v.at[rows(c * 8 + me, 2 * N), :],
            send_sem=send4.at[c, r], recv_sem=recv4.at[c, r], device_id=member(to), device_id_type=MESH)

    agg_v[...] = jnp.zeros_like(agg_v)
    total_v[...] = jnp.zeros_like(total_v)
    proj_v[...] = jnp.zeros_like(proj_v)
    for cp in ones[:2]:
        cp.wait()
    for q in range(E // LANES):
        g, j, cols = q // J, q % J, slice(q * LANES, (q + 1) * LANES)
        wch_v[g, pl.ds(j, KW, stride=J), :] = cw_v[:, cols]
        wch_v[g, KW * J + j:KW * J + j + 1, :] = cb_v[:, cols]

    def conv_tokens(g, k):
        w = [wch_v[g, i * J:(i + 1) * J, :] for i in range(KW + 1)]
        for tt in range(16):
            r = pl.multiple_of((k * 16 + tt) * J, J)
            acc = w[KW]
            for i in range(KW):
                acc = acc + w[i] * xch_v[g, pl.ds(r + (HALO - KW + 1 + i) * J, J), :]
            dch_v[0, pl.ds(r, J), :] = silu(acc)

    def conv_later(g):
        @pl.when(g + AHEAD < G)
        def _():
            in_copy(1, g + AHEAD).start()

        in_copy(0, g).wait()
        for j in range(J):
            xch_v[g, pl.ds(HALO * J + j, T, stride=J), :] = x_v[g, :, j * LANES:(j + 1) * LANES].astype(f32)

        def tokens(k, _):
            conv_tokens(g, k)
            return 0

        lax.fori_loop(1, T // 16, tokens, 0)
        for j in range(J):
            late = dch_v[0, pl.ds(16 * J + j, T - 16, stride=J), :]
            u_v[g, 16:T, j * LANES:(j + 1) * LANES] = late.astype(bf16)

    def conv_first(g, _):
        in_copy(2, g).start()
        halo_copy(g).wait_recv()
        for j in range(J):
            halo = halo_v[g, :, j * LANES:(j + 1) * LANES].astype(f32)
            xch_v[g, pl.ds(j, HALO, stride=J), :] = jnp.where(line > 0, halo, 0.0)
        conv_tokens(g, 0)
        for j in range(J):
            u_v[g, 0:16, j * LANES:(j + 1) * LANES] = dch_v[0, pl.ds(j, 16, stride=J), :].astype(bf16)
        in_copy(1, g).wait()
        proj_v[...] += lax.dot_general(u_v[g], xp_v[g], (((1,), (1,)), ((), ())), preferred_element_type=f32)
        return 0

    conv_later(0)
    pl.semaphore_wait(barrier, 24)
    for g in range(G):
        halo_copy(g).start()

    def rest(g, _):
        conv_later(g)
        return 0

    lax.fori_loop(1, G, rest, 0)
    for cp in ones[2:]:
        cp.wait()
    for q in range(E // LANES):
        ach_v[q // J, pl.ds(q % J, N, stride=J), :] = a_v[:, q * LANES:(q + 1) * LANES] * -LOG2E
    lax.fori_loop(0, G, conv_first, 0)

    row = lax.broadcasted_iota(jnp.int32, (256, 16), 0)
    col = lax.broadcasted_iota(jnp.int32, (256, 16), 1)
    repeat = (row // N == col).astype(bf16)
    row = lax.broadcasted_iota(jnp.int32, (256, 96), 0)
    col = lax.broadcasted_iota(jnp.int32, (256, 96), 1)
    own = row % N == col % N
    row = lax.broadcasted_iota(jnp.int32, (96, 256), 0)
    col = lax.broadcasted_iota(jnp.int32, (96, 256), 1)
    gather = (row // 48 == col // LANES).astype(bf16)

    def spread(k, _):
        r = pl.multiple_of(k * 16, 16)
        b = proj_v[pl.ds(r, 16), R:R + N]
        c = proj_v[pl.ds(r, 16), R + N:R + 2 * N]
        parts = jnp.concatenate([*split3(b), *split3(c)], axis=1).astype(bf16)
        wide = jnp.dot(repeat, parts, preferred_element_type=f32)
        wide = jnp.where(own, wide, 0.0).astype(bf16)
        full = jnp.dot(wide, gather, preferred_element_type=f32)
        r = pl.multiple_of(k * 256, 256)
        bs_v[pl.ds(r, 256), :] = full[:, :LANES]
        cs_v[pl.ds(r, 256), :] = full[:, LANES:]
        return 0

    lax.fori_loop(0, T // 16, spread, 0, unroll=True)

    def steps_of(g, slot):
        off = pl.multiple_of(g * GW, GW)
        in_copy(2, g).wait()
        dt_low = proj_v[:, 0:R].astype(bf16)
        for s in range(0, GW, 256):
            v = jnp.dot(dt_low, dp_v[g, :, s:s + 256], preferred_element_type=f32)
            d = softplus_clipped(v + db_v[:, pl.ds(off + s, 256)])
            i = d * u_v[g, :, s:s + 256].astype(f32)
            for h in range(2):
                j = s // LANES + h
                dch_v[slot, pl.ds(j, T, stride=J), :] = d[:, h * LANES:(h + 1) * LANES]
                ich_v[slot, pl.ds(j, T, stride=J), :] = i[:, h * LANES:(h + 1) * LANES]

    def recur(g, slot, h, cum, unroll, emit):
        def steps(k, carry):
            h, cum = list(carry[0]), carry[1]
            for tt in range(unroll):
                t = k * unroll + tt
                r = pl.multiple_of(t * J, J)
                d = dch_v[slot, pl.ds(r, J), :]
                i = ich_v[slot, pl.ds(r, J), :]
                if cum is not None:
                    cum = cum + d
                ys = []
                for n in range(N):
                    e = jnp.exp2(d * ach_v[g, n * J:(n + 1) * J, :])
                    b = bs_v[pl.ds(t * N + n, J, stride=0), :]
                    h[n] = e * h[n] + b * i
                    if emit is not None:
                        ys.append(cs_v[pl.ds(t * N + n, J, stride=0), :] * h[n])
                        if n % 4 == 3:
                            y4 = (ys[0] + ys[1]) + (ys[2] + ys[3])
                            y_t = y4 if n == 3 else y_t + y4
                            ys = []
                if emit is not None:
                    emit(r, y_t, cum)
            return tuple(h), cum

        return lax.fori_loop(0, T // unroll, steps, (tuple(h), cum))

    zero = jnp.zeros((J, LANES), f32)

    def aggregate(c, half, h, cum):
        for n in range(N):
            agg_v[pl.ds(c * (J * AGG) + half * N + n, J, stride=AGG), :] = h[n]
        agg_v[pl.ds(c * (J * AGG) + 2 * N + half, J, stride=AGG), :] = cum

    def carried(c, half, n):
        return carry_v[pl.ds(c * (J * 2 * N) + half * N + n, J, stride=2 * N), :]

    def final_state(p, half):
        g = 2 * p + half
        steps_of(g, g)
        aggregate(p, half, *recur(g, g, (zero,) * N, zero, UNROLL_S, None))

    def from_zero(p, half):
        g = 2 * p + half
        steps_of(g, G // 2)

        def emit(r, y_t, cum):
            ych_v[g, pl.ds(r, J), :] = y_t
            cch_v[g - G // 2, pl.ds(r, J), :] = cum

        aggregate(p, half, *recur(g, G // 2, (zero,) * N, zero, UNROLL_L, emit))

    def rates(c, half):
        col = pl.multiple_of((c * 2 + half) * GW + me * LANES, LANES)
        return a_v[:, pl.ds(col, LANES)] * -LOG2E

    def advance(state, ref, slot, rate, half):
        d = ref[pl.ds(slot * AGG + 2 * N + half, N, stride=0), :]
        return jnp.exp2(d * rate) * state + ref[pl.ds(pl.multiple_of(slot * AGG + half * N, 8), N), :]

    def dsums(ref, slot):
        return ref[pl.ds(pl.multiple_of(slot * AGG + 2 * N, 8), 8), :]

    def put(ref, slot, row, count, value):
        ref[pl.ds(pl.multiple_of(slot * AGG + row, 8), count), :] = value

    def send_first(c):
        got_v[rows(c * 8 + me, AGG), :] = agg_v[rows(c * 8 + me, AGG), :]
        for r in range(1, 8):
            first_copy(c, r).start()

    def after_first(c):
        for r in range(1, 8):
            first_copy(c, r).wait_recv()
        d = dsums(got_v, c * 8)
        for k in range(1, 8):
            d = d + dsums(got_v, c * 8 + k)
        put(total_v, c, 2 * N, 8, d)
        put(all_v, c * 16 + mine, 2 * N, 8, d)
        for half in range(2):
            rate = rates(c, half)
            s = jnp.zeros((N, LANES), f32)
            for k in range(8):
                s = advance(s, got_v, c * 8 + k, rate, half)
            put(total_v, c, half * N, N, s)
            put(all_v, c * 16 + mine, half * N, N, s)
        for r in range(1, 16):
            group_copy(c, r).start()

    def after_group(c):
        for r in range(1, 16):
            group_copy(c, r).wait_recv()
        for half in range(2):
            rate = rates(c, half)
            s = jnp.zeros((N, LANES), f32)
            before_mine = s
            for k in range(15):
                s = advance(s, all_v, c * 16 + k, rate, half)
                before_mine = jnp.where(mine > k, s, before_mine)
            s = before_mine
            for k in range(8):
                back_v[pl.ds(pl.multiple_of((c * 8 + k) * 2 * N + half * N, 8), N), :] = s
                if k < 7:
                    s = advance(s, got_v, c * 8 + k, rate, half)
        carry_v[rows(c * 8 + me, 2 * N), :] = back_v[rows(c * 8 + me, 2 * N), :]
        for r in range(1, 8):
            last_copy(c, r).start()

    def out_copy(g):
        cols = pl.ds(pl.multiple_of(g * GW, GW), GW)
        return pltpu.make_async_copy(out_v.at[g], out_hbm.at[:, cols], out_sem.at[g])

    def finish(g):
        off = pl.multiple_of(g * GW, GW)
        for j in range(J):
            cols = slice(j * LANES, (j + 1) * LANES)
            y_t = ych_v[g, pl.ds(j, T, stride=J), :]
            out_v[g, :, cols] = y_t + sk_v[:, pl.ds(off + j * LANES, LANES)] * u_v[g, :, cols].astype(f32)
        out_copy(g).start()

    def wait_carry(c):
        for r in range(1, 8):
            last_copy(c, r).wait_recv()

    def from_carry(p, half):
        c = p - C
        g = 2 * c + half
        if half == 0:
            wait_carry(c)

        def emit(r, y_t, cum):
            ych_v[g, pl.ds(r, J), :] = y_t

        recur(g, g, [carried(c, half, n) for n in range(N)], None, UNROLL_F, emit)
        finish(g)

    def add_carry(p, half):
        c = p - C
        g = 2 * c + half
        if half == 0:
            wait_carry(c)
        hch_v = dch_v.at[0, pl.ds(0, N * J), :]
        for n in range(N):
            hch_v[n * J:(n + 1) * J, :] = carried(c, half, n)

        def steps(k, _):
            for tt in range(UNROLL_C):
                t = k * UNROLL_C + tt
                r = pl.multiple_of(t * J, J)
                cum = cch_v[g - G // 2, pl.ds(r, J), :]
                y_t = ych_v[g, pl.ds(r, J), :]
                for n4 in range(0, N, 4):
                    part = []
                    for n in range(n4, n4 + 4):
                        e = jnp.exp2(cum * ach_v[g, n * J:(n + 1) * J, :])
                        c_n = cs_v[pl.ds(t * N + n, J, stride=0), :]
                        part.append(c_n * (e * hch_v[n * J:(n + 1) * J, :]))
                    y_t = y_t + ((part[0] + part[1]) + (part[2] + part[3]))
                ych_v[g, pl.ds(r, J), :] = y_t
            return 0

        lax.fori_loop(0, T // UNROLL_C, steps, 0)
        finish(g)

    def pair(work, lo, hi):
        def body(p, _):
            work(p, 0)
            work(p, 1)
            if hi <= C:
                send_first(p)
            if hi > 1 and lo <= C:
                pl.when((p >= 1) & (p <= C))(lambda: after_first(p - 1))
            if hi > 2 and lo < C + 2:
                pl.when((p >= 2) & (p < C + 2))(lambda: after_group(p - 2))
            return 0

        lax.fori_loop(lo, hi, body, 0)

    pair(final_state, 0, C // 2)
    pair(from_zero, C // 2, C)
    pair(from_carry, C, C + C // 2)
    pair(add_carry, C + C // 2, 2 * C)

    for c in range(C):
        for r in range(1, 8):
            first_copy(c, r).wait_send()
            last_copy(c, r).wait_send()
        for r in range(1, 16):
            group_copy(c, r).wait_send()
    for g in range(G):
        halo_copy(g).wait_send()
        out_copy(g).wait()


ANY = pl.BlockSpec(memory_space=pl.ANY)
UNROLL_S, UNROLL_L, UNROLL_F, UNROLL_C = 16, 16, 16, 16
AHEAD = 3


def local(x_in, gate_in, conv_weight, conv_bias, x_proj, dt_proj, dt_bias, decay_rates, skip_gain):
    vmem, dma = pltpu.VMEM, pltpu.SemaphoreType.DMA
    y = pl.pallas_call(
        kernel,
        name="selective_scan",
        out_shape=pltpu.VMEM((T, E), f32),
        in_specs=[ANY] * 8,
        out_specs=ANY,
        scratch_shapes=[
            vmem((G, T, GW), bf16), vmem((KW, E), f32), vmem((1, E), f32),
            vmem((G, R + 2 * N, GW), bf16), vmem((G, R, GW), bf16), vmem((1, E), f32), vmem((N, E), f32), vmem((1, E), f32),
            vmem((G, HALO, GW), bf16), vmem((G, (HALO + T) * J, LANES), f32), vmem((G, (KW + 1) * J, LANES), f32),
            vmem((G, T, GW), bf16), vmem((T * N, LANES), f32), vmem((T * N, LANES), f32), vmem((G, N * J, LANES), f32),
            vmem((T, R + 2 * N), f32), vmem((G // 2 + 1, ROWS, LANES), f32), vmem((G // 2 + 1, ROWS, LANES), f32),
            vmem((G, ROWS, LANES), f32), vmem((G // 2, ROWS, LANES), f32), vmem((G, T, GW), f32),
            vmem((C * 8 * AGG, LANES), f32), vmem((C * 8 * AGG, LANES), f32), vmem((C * AGG, LANES), f32),
            vmem((C * 16 * AGG, LANES), f32), vmem((C * 8 * 2 * N, LANES), f32), vmem((C * 8 * 2 * N, LANES), f32),
            dma((3, G)), dma((5,)), dma((G,)), dma((G,)), dma((G,)),
            dma((C, 8)), dma((C, 8)), dma((C, 16)), dma((C, 16)), dma((C, 8)), dma((C, 8))],
        compiler_params=pltpu.CompilerParams(collective_id=0, has_side_effects=True, vmem_limit_bytes=52 * 2**20),
    )(*(pltpu.with_memory_space_constraint(v, pltpu.HBM) for v in (
        x_in, conv_weight, conv_bias.reshape(1, E), x_proj.T, dt_proj, dt_bias.reshape(1, E), decay_rates,
        skip_gain.reshape(1, E))))
    gate = gate_in.astype(f32)
    return (y * (gate * (0.5 * jnp.tanh(0.5 * gate) + 0.5))).astype(bf16)


def solution(mesh):
    tokens = P(("outer", "inner"), None)
    return jax.shard_map(
        local, mesh=mesh, in_specs=(tokens, tokens, P(), P(), P(), P(), P(), P(), P()),
        out_specs=tokens, check_vma=False)
```

```python
import math

import jax
import jax.numpy as jnp
from jax import lax
from jax.experimental import pallas as pl
from jax.experimental.pallas import tpu as pltpu
from jax.sharding import PartitionSpec as P

f32, bf16 = jnp.float32, jnp.bfloat16
MESH = pl.DeviceIdType.MESH
LOG2E = math.log2(math.e)
LN2 = math.log(2.0)
DT_CEILING = 0.25

T = 128
E = 8192
N = 16
R = 256
KW = 4
LANES = 128
J = 8
GW = J * LANES
G = E // GW
ROWS = T * J
C = G // 2
AGG = 40
HALO = 16


def silu(v):
    d = 1.0 + jnp.exp2(v * -LOG2E)
    r = pl.reciprocal(d, approx=True)
    r = r * (2.0 - d * r)
    return v * r


def softplus_clipped(v):
    z = jnp.exp2(jnp.minimum(v, 0.0) * LOG2E)
    small = z * (1.0 - z * (0.5 - z * (1.0 / 3.0 - 0.25 * z)))
    big = jnp.log2(1.0 + z) * LN2
    return jnp.minimum(jnp.where(z < 0.03, small, big), DT_CEILING)


def split3(v):
    hi = v.astype(bf16).astype(f32)
    mid = (v - hi).astype(bf16).astype(f32)
    lo = (v - hi - mid).astype(bf16).astype(f32)
    return hi, mid, lo


def kernel(x_hbm, cw_hbm, cb_hbm, xp_hbm, dp_hbm, db_hbm, a_hbm, sk_hbm, out_hbm,
           x_v, cw_v, cb_v, xp_v, dp_v, db_v, a_v, sk_v, halo_v, xch_v, wch_v, u_v, bs_v, cs_v, ach_v,
           proj_v, dch_v, ich_v, ych_v, cch_v, out_v,
           agg_v, got_v, total_v, all_v, back_v, carry_v,
           in_sem, one_sem, out_sem, hsend, hrecv, send1, recv1, send2, recv2, send4, recv4):
    outer, x = lax.axis_index("outer"), lax.axis_index("inner")
    core, mine = outer % 2, outer // 2
    me = core * 4 + x
    line = outer * 4 + x

    def in_copy(kind, g):
        cols = pl.ds(pl.multiple_of(g * GW, GW), GW)
        source, target = ((x_hbm, x_v), (xp_hbm, xp_v), (dp_hbm, dp_v))[kind]
        return pltpu.make_async_copy(source.at[:, cols], target.at[g], in_sem.at[kind, g])

    ones = [pltpu.make_async_copy(s, t, one_sem.at[k]) for k, (s, t) in enumerate(
        ((cw_hbm, cw_v), (cb_hbm, cb_v), (a_hbm, a_v), (db_hbm, db_v), (sk_hbm, sk_v)))]
    for cp in ones[:2]:
        cp.start()
    for g in range(G):
        in_copy(0, g).start()
    for cp in ones[2:]:
        cp.start()
    for g in range(AHEAD):
        in_copy(1, g).start()

    def at_line(v):
        return (v // 4, v % 4)

    def member(m):
        return (mine * 2 + m // 4, m % 4)

    def peer(v):
        return (v * 2 + core, x)

    devices = lax.axis_size("outer") * lax.axis_size("inner")
    barrier = pltpu.get_barrier_semaphore()
    after, before = (line + 1) % devices, (line + devices - 1) % devices
    pl.semaphore_signal(barrier, inc=1, device_id=at_line(after), device_id_type=MESH)
    pl.semaphore_signal(barrier, inc=1, device_id=at_line(before), device_id_type=MESH)
    for r in range(1, 8):
        pl.semaphore_signal(barrier, inc=1, device_id=member((me + r) % 8), device_id_type=MESH)
    for r in range(1, 16):
        pl.semaphore_signal(barrier, inc=1, device_id=peer((mine + r) % 16), device_id_type=MESH)

    def halo_copy(g):
        cols = pl.ds(pl.multiple_of(g * GW, GW), GW)
        return pltpu.make_async_remote_copy(
            src_ref=x_hbm.at[pl.ds(T - HALO, HALO), cols], dst_ref=halo_v.at[g], send_sem=hsend.at[g],
            recv_sem=hrecv.at[g], device_id=at_line(after), device_id_type=MESH)

    def rows(index, count):
        return pl.ds(pl.multiple_of(index * count, 8), count)

    def first_copy(c, r):
        to = (me + r) % 8
        return pltpu.make_async_remote_copy(
            src_ref=agg_v.at[rows(c * 8 + to, AGG), :], dst_ref=got_v.at[rows(c * 8 + me, AGG), :],
            send_sem=send1.at[c, r], recv_sem=recv1.at[c, r], device_id=member(to), device_id_type=MESH)

    def group_copy(c, r):
        return pltpu.make_async_remote_copy(
            src_ref=total_v.at[rows(c, AGG), :], dst_ref=all_v.at[rows(c * 16 + mine, AGG), :],
            send_sem=send2.at[c, r], recv_sem=recv2.at[c, r], device_id=peer((mine + r) % 16), device_id_type=MESH)

    def last_copy(c, r):
        to = (me + r) % 8
        return pltpu.make_async_remote_copy(
            src_ref=back_v.at[rows(c * 8 + to, 2 * N), :], dst_ref=carry_v.at[rows(c * 8 + me, 2 * N), :],
            send_sem=send4.at[c, r], recv_sem=recv4.at[c, r], device_id=member(to), device_id_type=MESH)

    agg_v[...] = jnp.zeros_like(agg_v)
    total_v[...] = jnp.zeros_like(total_v)
    proj_v[...] = jnp.zeros_like(proj_v)
    for cp in ones[:2]:
        cp.wait()
    for q in range(E // LANES):
        g, j, cols = q // J, q % J, slice(q * LANES, (q + 1) * LANES)
        wch_v[g, pl.ds(j, KW, stride=J), :] = cw_v[:, cols]
        wch_v[g, KW * J + j:KW * J + j + 1, :] = cb_v[:, cols]

    def conv_tokens(g, k, slot=0):
        w = [wch_v[g, i * J:(i + 1) * J, :] for i in range(KW + 1)]
        for tt in range(16):
            r = pl.multiple_of((k * 16 + tt) * J, J)
            acc = w[KW]
            for i in range(KW):
                acc = acc + w[i] * xch_v[g, pl.ds(r + (HALO - KW + 1 + i) * J, J), :]
            dch_v[slot, pl.ds(r, J), :] = silu(acc)

    def conv_later(g):
        @pl.when(g + AHEAD < G)
        def _():
            in_copy(1, g + AHEAD).start()

        in_copy(0, g).wait()
        for j in range(J):
            xch_v[g, pl.ds(HALO * J + j, T, stride=J), :] = x_v[g, :, j * LANES:(j + 1) * LANES].astype(f32)

        def tokens(k, _):
            conv_tokens(g, k)
            return 0

        lax.fori_loop(1, T // 16, tokens, 0)
        for j in range(J):
            late = dch_v[0, pl.ds(16 * J + j, T - 16, stride=J), :]
            u_v[g, 16:T, j * LANES:(j + 1) * LANES] = late.astype(bf16)

    def conv_first(pair_of_groups, _):
        two = [(2 * pair_of_groups + slot, slot) for slot in range(2)]
        for g, slot in two:
            in_copy(2, g).start()
            halo_copy(g).wait_recv()
            in_copy(1, g).wait()
        for g, slot in two:
            for j in range(J):
                halo = halo_v[g, :, j * LANES:(j + 1) * LANES].astype(f32)
                xch_v[g, pl.ds(j, HALO, stride=J), :] = jnp.where(line > 0, halo, 0.0)
            conv_tokens(g, 0, slot)
            for j in range(J):
                early = dch_v[slot, pl.ds(j, 16, stride=J), :]
                u_v[g, 0:16, j * LANES:(j + 1) * LANES] = early.astype(bf16)
        proj = [lax.dot_general(u_v[g], xp_v[g], (((1,), (1,)), ((), ())), preferred_element_type=f32)
                for g, slot in two]
        proj_v[...] += proj[0] + proj[1]
        return 0

    conv_later(0)
    pl.semaphore_wait(barrier, 24)
    for g in range(G):
        halo_copy(g).start()

    def rest(g, _):
        conv_later(g)
        return 0

    lax.fori_loop(1, G, rest, 0)
    for cp in ones[2:]:
        cp.wait()
    for q in range(E // LANES):
        ach_v[q // J, pl.ds(q % J, N, stride=J), :] = a_v[:, q * LANES:(q + 1) * LANES] * -LOG2E
    lax.fori_loop(0, G // 2, conv_first, 0)

    row = lax.broadcasted_iota(jnp.int32, (256, 16), 0)
    col = lax.broadcasted_iota(jnp.int32, (256, 16), 1)
    repeat = (row // N == col).astype(bf16)
    row = lax.broadcasted_iota(jnp.int32, (256, 96), 0)
    col = lax.broadcasted_iota(jnp.int32, (256, 96), 1)
    own = row % N == col % N
    row = lax.broadcasted_iota(jnp.int32, (96, 256), 0)
    col = lax.broadcasted_iota(jnp.int32, (96, 256), 1)
    gather = (row // 48 == col // LANES).astype(bf16)

    def spread(k, _):
        r = pl.multiple_of(k * 16, 16)
        b = proj_v[pl.ds(r, 16), R:R + N]
        c = proj_v[pl.ds(r, 16), R + N:R + 2 * N]
        parts = jnp.concatenate([*split3(b), *split3(c)], axis=1).astype(bf16)
        wide = jnp.dot(repeat, parts, preferred_element_type=f32)
        wide = jnp.where(own, wide, 0.0).astype(bf16)
        full = jnp.dot(wide, gather, preferred_element_type=f32)
        r = pl.multiple_of(k * 256, 256)
        bs_v[pl.ds(r, 256), :] = full[:, :LANES]
        cs_v[pl.ds(r, 256), :] = full[:, LANES:]
        return 0

    lax.fori_loop(0, T // 16, spread, 0, unroll=True)

    def steps_of(g, slot):
        off = pl.multiple_of(g * GW, GW)
        in_copy(2, g).wait()
        dt_low = proj_v[:, 0:R].astype(bf16)
        for s in range(0, GW, 256):
            v = jnp.dot(dt_low, dp_v[g, :, s:s + 256], preferred_element_type=f32)
            d = softplus_clipped(v + db_v[:, pl.ds(off + s, 256)])
            i = d * u_v[g, :, s:s + 256].astype(f32)
            for h in range(2):
                j = s // LANES + h
                dch_v[slot, pl.ds(j, T, stride=J), :] = d[:, h * LANES:(h + 1) * LANES]
                ich_v[slot, pl.ds(j, T, stride=J), :] = i[:, h * LANES:(h + 1) * LANES]

    def recur(g, slot, h, cum, unroll, emit):
        def steps(k, carry):
            h, cum = list(carry[0]), carry[1]
            for tt in range(unroll):
                t = k * unroll + tt
                r = pl.multiple_of(t * J, J)
                d = dch_v[slot, pl.ds(r, J), :]
                i = ich_v[slot, pl.ds(r, J), :]
                if cum is not None:
                    cum = cum + d
                ys = []
                for n in range(N):
                    e = jnp.exp2(d * ach_v[g, n * J:(n + 1) * J, :])
                    b = bs_v[pl.ds(t * N + n, J, stride=0), :]
                    h[n] = e * h[n] + b * i
                    if emit is not None:
                        ys.append(cs_v[pl.ds(t * N + n, J, stride=0), :] * h[n])
                        if n % 4 == 3:
                            y4 = (ys[0] + ys[1]) + (ys[2] + ys[3])
                            y_t = y4 if n == 3 else y_t + y4
                            ys = []
                if emit is not None:
                    emit(r, y_t, cum)
            return tuple(h), cum

        return lax.fori_loop(0, T // unroll, steps, (tuple(h), cum))

    zero = jnp.zeros((J, LANES), f32)

    def aggregate(c, half, h, cum):
        for n in range(N):
            agg_v[pl.ds(c * (J * AGG) + half * N + n, J, stride=AGG), :] = h[n]
        agg_v[pl.ds(c * (J * AGG) + 2 * N + half, J, stride=AGG), :] = cum

    def carried(c, half, n):
        return carry_v[pl.ds(c * (J * 2 * N) + half * N + n, J, stride=2 * N), :]

    def final_state(p, half):
        g = 2 * p + half
        steps_of(g, g)
        aggregate(p, half, *recur(g, g, (zero,) * N, zero, UNROLL_S, None))

    def from_zero(p, half):
        g = 2 * p + half
        steps_of(g, G // 2)

        def emit(r, y_t, cum):
            ych_v[g, pl.ds(r, J), :] = y_t
            cch_v[g - G // 2, pl.ds(r, J), :] = cum

        aggregate(p, half, *recur(g, G // 2, (zero,) * N, zero, UNROLL_L, emit))

    def rates(c, half):
        col = pl.multiple_of((c * 2 + half) * GW + me * LANES, LANES)
        return a_v[:, pl.ds(col, LANES)] * -LOG2E

    def advance(state, ref, slot, rate, half):
        d = ref[pl.ds(slot * AGG + 2 * N + half, N, stride=0), :]
        return jnp.exp2(d * rate) * state + ref[pl.ds(pl.multiple_of(slot * AGG + half * N, 8), N), :]

    def dsums(ref, slot):
        return ref[pl.ds(pl.multiple_of(slot * AGG + 2 * N, 8), 8), :]

    def put(ref, slot, row, count, value):
        ref[pl.ds(pl.multiple_of(slot * AGG + row, 8), count), :] = value

    def send_first(c):
        got_v[rows(c * 8 + me, AGG), :] = agg_v[rows(c * 8 + me, AGG), :]
        for r in range(1, 8):
            first_copy(c, r).start()

    def after_first(c):
        for r in range(1, 8):
            first_copy(c, r).wait_recv()
        d = dsums(got_v, c * 8)
        for k in range(1, 8):
            d = d + dsums(got_v, c * 8 + k)
        put(total_v, c, 2 * N, 8, d)
        put(all_v, c * 16 + mine, 2 * N, 8, d)
        for half in range(2):
            rate = rates(c, half)
            s = jnp.zeros((N, LANES), f32)
            for k in range(8):
                s = advance(s, got_v, c * 8 + k, rate, half)
            put(total_v, c, half * N, N, s)
            put(all_v, c * 16 + mine, half * N, N, s)
        for r in range(1, 16):
            group_copy(c, r).start()

    def after_group(c):
        for r in range(1, 16):
            group_copy(c, r).wait_recv()
        for half in range(2):
            rate = rates(c, half)
            s = jnp.zeros((N, LANES), f32)
            before_mine = s
            for k in range(15):
                s = advance(s, all_v, c * 16 + k, rate, half)
                before_mine = jnp.where(mine > k, s, before_mine)
            s = before_mine
            for k in range(8):
                back_v[pl.ds(pl.multiple_of((c * 8 + k) * 2 * N + half * N, 8), N), :] = s
                if k < 7:
                    s = advance(s, got_v, c * 8 + k, rate, half)
        carry_v[rows(c * 8 + me, 2 * N), :] = back_v[rows(c * 8 + me, 2 * N), :]
        for r in range(1, 8):
            last_copy(c, r).start()

    def out_copy(g):
        cols = pl.ds(pl.multiple_of(g * GW, GW), GW)
        return pltpu.make_async_copy(out_v.at[g], out_hbm.at[:, cols], out_sem.at[g])

    def finish(g):
        off = pl.multiple_of(g * GW, GW)
        for j in range(J):
            cols = slice(j * LANES, (j + 1) * LANES)
            y_t = ych_v[g, pl.ds(j, T, stride=J), :]
            out_v[g, :, cols] = y_t + sk_v[:, pl.ds(off + j * LANES, LANES)] * u_v[g, :, cols].astype(f32)
        out_copy(g).start()

    def wait_carry(c):
        for r in range(1, 8):
            last_copy(c, r).wait_recv()

    def from_carry(p, half):
        c = p - C
        g = 2 * c + half
        if half == 0:
            wait_carry(c)

        def emit(r, y_t, cum):
            ych_v[g, pl.ds(r, J), :] = y_t

        recur(g, g, [carried(c, half, n) for n in range(N)], None, UNROLL_F, emit)
        finish(g)

    def add_carry(p, half):
        c = p - C
        g = 2 * c + half
        if half == 0:
            wait_carry(c)
        hch_v = dch_v.at[0, pl.ds(0, N * J), :]
        for n in range(N):
            hch_v[n * J:(n + 1) * J, :] = carried(c, half, n)

        def steps(k, _):
            for tt in range(UNROLL_C):
                t = k * UNROLL_C + tt
                r = pl.multiple_of(t * J, J)
                cum = cch_v[g - G // 2, pl.ds(r, J), :]
                y_t = ych_v[g, pl.ds(r, J), :]
                for n4 in range(0, N, 4):
                    part = []
                    for n in range(n4, n4 + 4):
                        e = jnp.exp2(cum * ach_v[g, n * J:(n + 1) * J, :])
                        c_n = cs_v[pl.ds(t * N + n, J, stride=0), :]
                        part.append(c_n * (e * hch_v[n * J:(n + 1) * J, :]))
                    y_t = y_t + ((part[0] + part[1]) + (part[2] + part[3]))
                ych_v[g, pl.ds(r, J), :] = y_t
            return 0

        lax.fori_loop(0, T // UNROLL_C, steps, 0)
        finish(g)

    def pair(work, lo, hi):
        def body(p, _):
            work(p, 0)
            work(p, 1)
            if hi <= C:
                send_first(p)
            if hi > 1 and lo <= C:
                pl.when((p >= 1) & (p <= C))(lambda: after_first(p - 1))
            if hi > 2 and lo < C + 2:
                pl.when((p >= 2) & (p < C + 2))(lambda: after_group(p - 2))
            return 0

        lax.fori_loop(lo, hi, body, 0)

    pair(final_state, 0, C // 2)
    pair(from_zero, C // 2, C)
    pair(from_carry, C, C + C // 2)
    pair(add_carry, C + C // 2, 2 * C)

    for c in range(C):
        for r in range(1, 8):
            first_copy(c, r).wait_send()
            last_copy(c, r).wait_send()
        for r in range(1, 16):
            group_copy(c, r).wait_send()
    for g in range(G):
        halo_copy(g).wait_send()
        out_copy(g).wait()


ANY = pl.BlockSpec(memory_space=pl.ANY)
UNROLL_S, UNROLL_L, UNROLL_F, UNROLL_C = 16, 16, 16, 16
AHEAD = 3


def local(x_in, gate_in, conv_weight, conv_bias, x_proj, dt_proj, dt_bias, decay_rates, skip_gain):
    vmem, dma = pltpu.VMEM, pltpu.SemaphoreType.DMA
    y = pl.pallas_call(
        kernel,
        name="selective_scan",
        out_shape=pltpu.VMEM((T, E), f32),
        in_specs=[ANY] * 8,
        out_specs=ANY,
        scratch_shapes=[
            vmem((G, T, GW), bf16), vmem((KW, E), f32), vmem((1, E), f32),
            vmem((G, R + 2 * N, GW), bf16), vmem((G, R, GW), bf16), vmem((1, E), f32), vmem((N, E), f32), vmem((1, E), f32),
            vmem((G, HALO, GW), bf16), vmem((G, (HALO + T) * J, LANES), f32), vmem((G, (KW + 1) * J, LANES), f32),
            vmem((G, T, GW), bf16), vmem((T * N, LANES), f32), vmem((T * N, LANES), f32), vmem((G, N * J, LANES), f32),
            vmem((T, R + 2 * N), f32), vmem((G // 2 + 1, ROWS, LANES), f32), vmem((G // 2 + 1, ROWS, LANES), f32),
            vmem((G, ROWS, LANES), f32), vmem((G // 2, ROWS, LANES), f32), vmem((G, T, GW), f32),
            vmem((C * 8 * AGG, LANES), f32), vmem((C * 8 * AGG, LANES), f32), vmem((C * AGG, LANES), f32),
            vmem((C * 16 * AGG, LANES), f32), vmem((C * 8 * 2 * N, LANES), f32), vmem((C * 8 * 2 * N, LANES), f32),
            dma((3, G)), dma((5,)), dma((G,)), dma((G,)), dma((G,)),
            dma((C, 8)), dma((C, 8)), dma((C, 16)), dma((C, 16)), dma((C, 8)), dma((C, 8))],
        compiler_params=pltpu.CompilerParams(collective_id=0, has_side_effects=True, vmem_limit_bytes=52 * 2**20),
    )(*(pltpu.with_memory_space_constraint(v, pltpu.HBM) for v in (
        x_in, conv_weight, conv_bias.reshape(1, E), x_proj.T, dt_proj, dt_bias.reshape(1, E), decay_rates,
        skip_gain.reshape(1, E))))
    gate = gate_in.astype(f32)
    return (y * (gate * (0.5 * jnp.tanh(0.5 * gate) + 0.5))).astype(bf16)


def solution(mesh):
    tokens = P(("outer", "inner"), None)
    return jax.shard_map(
        local, mesh=mesh, in_specs=(tokens, tokens, P(), P(), P(), P(), P(), P(), P()),
        out_specs=tokens, check_vma=False)
```

```python
import math

import jax
import jax.numpy as jnp
from jax import lax
from jax.experimental import pallas as pl
from jax.experimental.pallas import tpu as pltpu
from jax.sharding import PartitionSpec as P

f32, bf16 = jnp.float32, jnp.bfloat16
MESH = pl.DeviceIdType.MESH
LOG2E = math.log2(math.e)
LN2 = math.log(2.0)
DT_CEILING = 0.25

T = 128
E = 8192
N = 16
R = 256
KW = 4
LANES = 128
J = 8
GW = J * LANES
G = E // GW
ROWS = T * J
C = G // 2
AGG = 40
HALO = 16
WIRE = 48


def silu(v):
    d = 1.0 + jnp.exp2(v * -LOG2E)
    r = pl.reciprocal(d, approx=True)
    r = r * (2.0 - d * r)
    return v * r


def softplus_clipped(v):
    z = jnp.exp2(jnp.minimum(v, 0.0) * LOG2E)
    small = z * (1.0 - z * (0.5 - z * (1.0 / 3.0 - 0.25 * z)))
    big = jnp.log2(1.0 + z) * LN2
    return jnp.minimum(jnp.where(z < 0.03, small, big), DT_CEILING)


def split3(v):
    hi = v.astype(bf16).astype(f32)
    mid = (v - hi).astype(bf16).astype(f32)
    lo = (v - hi - mid).astype(bf16).astype(f32)
    return hi, mid, lo


def kernel(x_hbm, cw_hbm, cb_hbm, xp_hbm, dp_hbm, db_hbm, a_hbm, sk_hbm, out_hbm,
           x_v, cw_v, cb_v, xp_v, dp_v, db_v, a_v, sk_v, halo_v, xch_v, wch_v, u_v, bs_v, cs_v, ach_v,
           proj_v, dch_v, ich_v, ych_v, cch_v, out_v,
           agg_v, got_v, total_v, all_v, back_v, carry_v,
           in_sem, one_sem, out_sem, hsend, hrecv, send1, recv1, send2, recv2, send4, recv4):
    outer, x = lax.axis_index("outer"), lax.axis_index("inner")
    core, mine = outer % 2, outer // 2
    me = core * 4 + x
    line = outer * 4 + x

    def in_copy(kind, g):
        cols = pl.ds(pl.multiple_of(g * GW, GW), GW)
        source, target = ((x_hbm, x_v), (xp_hbm, xp_v), (dp_hbm, dp_v))[kind]
        return pltpu.make_async_copy(source.at[:, cols], target.at[g], in_sem.at[kind, g])

    ones = [pltpu.make_async_copy(s, t, one_sem.at[k]) for k, (s, t) in enumerate(
        ((cw_hbm, cw_v), (cb_hbm, cb_v), (a_hbm, a_v), (db_hbm, db_v), (sk_hbm, sk_v)))]
    for cp in ones[:2]:
        cp.start()
    for g in range(G):
        in_copy(0, g).start()
    for cp in ones[2:]:
        cp.start()
    for g in range(AHEAD):
        in_copy(1, g).start()

    def at_line(v):
        return (v // 4, v % 4)

    def member(m):
        return (mine * 2 + m // 4, m % 4)

    def peer(v):
        return (v * 2 + core, x)

    devices = lax.axis_size("outer") * lax.axis_size("inner")
    barrier = pltpu.get_barrier_semaphore()
    after, before = (line + 1) % devices, (line + devices - 1) % devices
    pl.semaphore_signal(barrier, inc=1, device_id=at_line(after), device_id_type=MESH)
    pl.semaphore_signal(barrier, inc=1, device_id=at_line(before), device_id_type=MESH)
    for r in range(1, 8):
        pl.semaphore_signal(barrier, inc=1, device_id=member((me + r) % 8), device_id_type=MESH)
    for r in range(1, 16):
        pl.semaphore_signal(barrier, inc=1, device_id=peer((mine + r) % 16), device_id_type=MESH)

    def halo_copy(g):
        cols = pl.ds(pl.multiple_of(g * GW, GW), GW)
        return pltpu.make_async_remote_copy(
            src_ref=x_hbm.at[pl.ds(T - HALO, HALO), cols], dst_ref=halo_v.at[g], send_sem=hsend.at[g],
            recv_sem=hrecv.at[g], device_id=at_line(after), device_id_type=MESH)

    def rows(index, count):
        return pl.ds(pl.multiple_of(index * count, 8), count)

    def wire(slot, row, count):
        return pl.ds(pl.multiple_of(slot * WIRE + row, 16), count)

    def first_copy(c, r):
        to = (me + r) % 8
        return pltpu.make_async_remote_copy(
            src_ref=agg_v.at[rows(c * 8 + to, AGG), :], dst_ref=got_v.at[rows(c * 8 + me, AGG), :],
            send_sem=send1.at[c, r], recv_sem=recv1.at[c, r], device_id=member(to), device_id_type=MESH)

    def group_copy(c, r):
        return pltpu.make_async_remote_copy(
            src_ref=total_v.at[wire(c, 0, WIRE), :], dst_ref=all_v.at[wire(c * 16 + mine, 0, WIRE), :],
            send_sem=send2.at[c, r], recv_sem=recv2.at[c, r], device_id=peer((mine + r) % 16), device_id_type=MESH)

    def last_copy(c, r):
        to = (me + r) % 8
        return pltpu.make_async_remote_copy(
            src_ref=back_v.at[rows(c * 8 + to, 2 * N), :], dst_ref=carry_v.at[rows(c * 8 + me, 2 * N), :],
            send_sem=send4.at[c, r], recv_sem=recv4.at[c, r], device_id=member(to), device_id_type=MESH)

    agg_v[...] = jnp.zeros_like(agg_v)
    total_v[...] = jnp.zeros_like(total_v)
    proj_v[...] = jnp.zeros_like(proj_v)
    for cp in ones[:2]:
        cp.wait()
    for q in range(E // LANES):
        g, j, cols = q // J, q % J, slice(q * LANES, (q + 1) * LANES)
        wch_v[g, pl.ds(j, KW, stride=J), :] = cw_v[:, cols]
        wch_v[g, KW * J + j:KW * J + j + 1, :] = cb_v[:, cols]

    def conv_tokens(g, k, slot=0):
        w = [wch_v[g, i * J:(i + 1) * J, :] for i in range(KW + 1)]
        for tt in range(16):
            r = pl.multiple_of((k * 16 + tt) * J, J)
            acc = w[KW]
            for i in range(KW):
                acc = acc + w[i] * xch_v[g, pl.ds(r + (HALO - KW + 1 + i) * J, J), :]
            dch_v[slot, pl.ds(r, J), :] = silu(acc)

    def conv_later(g):
        @pl.when(g + AHEAD < G)
        def _():
            in_copy(1, g + AHEAD).start()

        in_copy(0, g).wait()
        for j in range(J):
            xch_v[g, pl.ds(HALO * J + j, T, stride=J), :] = x_v[g, :, j * LANES:(j + 1) * LANES].astype(f32)

        def tokens(k, _):
            conv_tokens(g, k)
            return 0

        lax.fori_loop(1, T // 16, tokens, 0)
        for j in range(J):
            late = dch_v[0, pl.ds(16 * J + j, T - 16, stride=J), :]
            u_v[g, 16:T, j * LANES:(j + 1) * LANES] = late.astype(bf16)

    def conv_first(pair_of_groups, _):
        two = [(2 * pair_of_groups + slot, slot) for slot in range(2)]
        for g, slot in two:
            in_copy(2, g).start()
            halo_copy(g).wait_recv()
            in_copy(1, g).wait()
        for g, slot in two:
            for j in range(J):
                halo = halo_v[g, :, j * LANES:(j + 1) * LANES].astype(f32)
                xch_v[g, pl.ds(j, HALO, stride=J), :] = jnp.where(line > 0, halo, 0.0)
            conv_tokens(g, 0, slot)
            for j in range(J):
                early = dch_v[slot, pl.ds(j, 16, stride=J), :]
                u_v[g, 0:16, j * LANES:(j + 1) * LANES] = early.astype(bf16)
        proj = [lax.dot_general(u_v[g], xp_v[g], (((1,), (1,)), ((), ())), preferred_element_type=f32)
                for g, slot in two]
        proj_v[...] += proj[0] + proj[1]
        return 0

    conv_later(0)
    pl.semaphore_wait(barrier, 24)
    for g in range(G):
        halo_copy(g).start()

    def rest(g, _):
        conv_later(g)
        return 0

    lax.fori_loop(1, G, rest, 0)
    for cp in ones[2:]:
        cp.wait()
    for q in range(E // LANES):
        ach_v[q // J, pl.ds(q % J, N, stride=J), :] = a_v[:, q * LANES:(q + 1) * LANES] * -LOG2E
    lax.fori_loop(0, G // 2, conv_first, 0)

    row = lax.broadcasted_iota(jnp.int32, (256, 16), 0)
    col = lax.broadcasted_iota(jnp.int32, (256, 16), 1)
    repeat = (row // N == col).astype(bf16)
    row = lax.broadcasted_iota(jnp.int32, (256, 96), 0)
    col = lax.broadcasted_iota(jnp.int32, (256, 96), 1)
    own = row % N == col % N
    row = lax.broadcasted_iota(jnp.int32, (96, 256), 0)
    col = lax.broadcasted_iota(jnp.int32, (96, 256), 1)
    gather = (row // 48 == col // LANES).astype(bf16)

    def spread(k, _):
        r = pl.multiple_of(k * 16, 16)
        b = proj_v[pl.ds(r, 16), R:R + N]
        c = proj_v[pl.ds(r, 16), R + N:R + 2 * N]
        parts = jnp.concatenate([*split3(b), *split3(c)], axis=1).astype(bf16)
        wide = jnp.dot(repeat, parts, preferred_element_type=f32)
        wide = jnp.where(own, wide, 0.0).astype(bf16)
        full = jnp.dot(wide, gather, preferred_element_type=f32)
        r = pl.multiple_of(k * 256, 256)
        bs_v[pl.ds(r, 256), :] = full[:, :LANES]
        cs_v[pl.ds(r, 256), :] = full[:, LANES:]
        return 0

    lax.fori_loop(0, T // 16, spread, 0, unroll=True)

    def steps_of(g, slot):
        off = pl.multiple_of(g * GW, GW)
        in_copy(2, g).wait()
        dt_low = proj_v[:, 0:R].astype(bf16)
        for s in range(0, GW, 256):
            v = jnp.dot(dt_low, dp_v[g, :, s:s + 256], preferred_element_type=f32)
            d = softplus_clipped(v + db_v[:, pl.ds(off + s, 256)])
            i = d * u_v[g, :, s:s + 256].astype(f32)
            for h in range(2):
                j = s // LANES + h
                dch_v[slot, pl.ds(j, T, stride=J), :] = d[:, h * LANES:(h + 1) * LANES]
                ich_v[slot, pl.ds(j, T, stride=J), :] = i[:, h * LANES:(h + 1) * LANES]

    def recur(g, slot, h, cum, unroll, emit):
        def steps(k, carry):
            h, cum = list(carry[0]), carry[1]
            for tt in range(unroll):
                t = k * unroll + tt
                r = pl.multiple_of(t * J, J)
                d = dch_v[slot, pl.ds(r, J), :]
                i = ich_v[slot, pl.ds(r, J), :]
                if cum is not None:
                    cum = cum + d
                ys = []
                for n in range(N):
                    e = jnp.exp2(d * ach_v[g, n * J:(n + 1) * J, :])
                    b = bs_v[pl.ds(t * N + n, J, stride=0), :]
                    h[n] = e * h[n] + b * i
                    if emit is not None:
                        ys.append(cs_v[pl.ds(t * N + n, J, stride=0), :] * h[n])
                        if n % 4 == 3:
                            y4 = (ys[0] + ys[1]) + (ys[2] + ys[3])
                            y_t = y4 if n == 3 else y_t + y4
                            ys = []
                if emit is not None:
                    emit(r, y_t, cum)
            return tuple(h), cum

        return lax.fori_loop(0, T // unroll, steps, (tuple(h), cum))

    zero = jnp.zeros((J, LANES), f32)

    def aggregate(c, half, h, cum):
        for n in range(N):
            agg_v[pl.ds(c * (J * AGG) + half * N + n, J, stride=AGG), :] = h[n]
        agg_v[pl.ds(c * (J * AGG) + 2 * N + half, J, stride=AGG), :] = cum

    def carried(c, half, n):
        return carry_v[pl.ds(c * (J * 2 * N) + half * N + n, J, stride=2 * N), :]

    def final_state(p, half):
        g = 2 * p + half
        steps_of(g, g)
        aggregate(p, half, *recur(g, g, (zero,) * N, zero, UNROLL_S, None))

    def from_zero(p, half):
        g = 2 * p + half
        steps_of(g, G // 2)

        def emit(r, y_t, cum):
            ych_v[g, pl.ds(r, J), :] = y_t
            cch_v[g - G // 2, pl.ds(r, J), :] = cum

        aggregate(p, half, *recur(g, G // 2, (zero,) * N, zero, UNROLL_L, emit))

    def rates(c, half):
        col = pl.multiple_of((c * 2 + half) * GW + me * LANES, LANES)
        return a_v[:, pl.ds(col, LANES)] * -LOG2E

    def advance(state, ref, slot, rate, half):
        d = ref[pl.ds(slot * AGG + 2 * N + half, N, stride=0), :]
        return jnp.exp2(d * rate) * state + ref[pl.ds(pl.multiple_of(slot * AGG + half * N, 8), N), :]

    def dsums(ref, slot):
        return ref[pl.ds(pl.multiple_of(slot * AGG + 2 * N, 8), 8), :]

    def send_first(c):
        got_v[rows(c * 8 + me, AGG), :] = agg_v[rows(c * 8 + me, AGG), :]
        for r in range(1, 8):
            first_copy(c, r).start()

    def after_first(c):
        for r in range(1, 8):
            first_copy(c, r).wait_recv()
        d = dsums(got_v, c * 8)
        for k in range(1, 8):
            d = d + dsums(got_v, c * 8 + k)
        d = jnp.concatenate([part[0:2] for part in split3(d)] + [jnp.zeros((10, LANES), f32)], axis=0).astype(bf16)
        total_v[wire(c, 2 * N, N), :] = d
        all_v[wire(c * 16 + mine, 2 * N, N), :] = d
        for half in range(2):
            rate = rates(c, half)
            s = jnp.zeros((N, LANES), f32)
            for k in range(8):
                s = advance(s, got_v, c * 8 + k, rate, half)
            total_v[wire(c, half * N, N), :] = s.astype(bf16)
            all_v[wire(c * 16 + mine, half * N, N), :] = s.astype(bf16)
        for r in range(1, 16):
            group_copy(c, r).start()

    def after_group(c):
        for r in range(1, 16):
            group_copy(c, r).wait_recv()
        for half in range(2):
            rate = rates(c, half)
            s = jnp.zeros((N, LANES), f32)
            before_mine = s
            for k in range(15):
                d = all_v[wire(c * 16 + k, 2 * N, N), :].astype(f32)
                d = d[half:half + 1] + d[2 + half:3 + half] + d[4 + half:5 + half]
                s = jnp.exp2(d * rate) * s + all_v[wire(c * 16 + k, half * N, N), :].astype(f32)
                before_mine = jnp.where(mine > k, s, before_mine)
            s = before_mine
            for k in range(8):
                back_v[pl.ds(pl.multiple_of((c * 8 + k) * 2 * N + half * N, 8), N), :] = s
                if k < 7:
                    s = advance(s, got_v, c * 8 + k, rate, half)
        carry_v[rows(c * 8 + me, 2 * N), :] = back_v[rows(c * 8 + me, 2 * N), :]
        for r in range(1, 8):
            last_copy(c, r).start()

    def out_copy(g):
        cols = pl.ds(pl.multiple_of(g * GW, GW), GW)
        return pltpu.make_async_copy(out_v.at[g], out_hbm.at[:, cols], out_sem.at[g])

    def finish(g):
        off = pl.multiple_of(g * GW, GW)
        for j in range(J):
            cols = slice(j * LANES, (j + 1) * LANES)
            y_t = ych_v[g, pl.ds(j, T, stride=J), :]
            out_v[g, :, cols] = y_t + sk_v[:, pl.ds(off + j * LANES, LANES)] * u_v[g, :, cols].astype(f32)
        out_copy(g).start()

    def wait_carry(c):
        for r in range(1, 8):
            last_copy(c, r).wait_recv()

    def from_carry(p, half):
        c = p - C
        g = 2 * c + half
        if half == 0:
            wait_carry(c)

        def emit(r, y_t, cum):
            ych_v[g, pl.ds(r, J), :] = y_t

        recur(g, g, [carried(c, half, n) for n in range(N)], None, UNROLL_F, emit)
        finish(g)

    def add_carry(p, half):
        c = p - C
        g = 2 * c + half
        if half == 0:
            wait_carry(c)
        hch_v = dch_v.at[0, pl.ds(0, N * J), :]
        for n in range(N):
            hch_v[n * J:(n + 1) * J, :] = carried(c, half, n)

        def steps(k, _):
            for tt in range(UNROLL_C):
                t = k * UNROLL_C + tt
                r = pl.multiple_of(t * J, J)
                cum = cch_v[g - G // 2, pl.ds(r, J), :]
                y_t = ych_v[g, pl.ds(r, J), :]
                for n4 in range(0, N, 4):
                    part = []
                    for n in range(n4, n4 + 4):
                        e = jnp.exp2(cum * ach_v[g, n * J:(n + 1) * J, :])
                        c_n = cs_v[pl.ds(t * N + n, J, stride=0), :]
                        part.append(c_n * (e * hch_v[n * J:(n + 1) * J, :]))
                    y_t = y_t + ((part[0] + part[1]) + (part[2] + part[3]))
                ych_v[g, pl.ds(r, J), :] = y_t
            return 0

        lax.fori_loop(0, T // UNROLL_C, steps, 0)
        finish(g)

    def pair(work, lo, hi):
        def body(p, _):
            work(p, 0)
            work(p, 1)
            if hi <= C:
                send_first(p)
            if hi > 1 and lo <= C:
                pl.when((p >= 1) & (p <= C))(lambda: after_first(p - 1))
            if hi > 2 and lo < C + 2:
                pl.when((p >= 2) & (p < C + 2))(lambda: after_group(p - 2))
            return 0

        lax.fori_loop(lo, hi, body, 0)

    pair(final_state, 0, C // 2)
    pair(from_zero, C // 2, C)
    pair(from_carry, C, C + C // 2)
    pair(add_carry, C + C // 2, 2 * C)

    for c in range(C):
        for r in range(1, 8):
            first_copy(c, r).wait_send()
            last_copy(c, r).wait_send()
        for r in range(1, 16):
            group_copy(c, r).wait_send()
    for g in range(G):
        halo_copy(g).wait_send()
        out_copy(g).wait()


ANY = pl.BlockSpec(memory_space=pl.ANY)
UNROLL_S, UNROLL_L, UNROLL_F, UNROLL_C = 16, 16, 16, 16
AHEAD = 3


def local(x_in, gate_in, conv_weight, conv_bias, x_proj, dt_proj, dt_bias, decay_rates, skip_gain):
    vmem, dma = pltpu.VMEM, pltpu.SemaphoreType.DMA
    y = pl.pallas_call(
        kernel,
        name="selective_scan",
        out_shape=pltpu.VMEM((T, E), f32),
        in_specs=[ANY] * 8,
        out_specs=ANY,
        scratch_shapes=[
            vmem((G, T, GW), bf16), vmem((KW, E), f32), vmem((1, E), f32),
            vmem((G, R + 2 * N, GW), bf16), vmem((G, R, GW), bf16), vmem((1, E), f32), vmem((N, E), f32), vmem((1, E), f32),
            vmem((G, HALO, GW), bf16), vmem((G, (HALO + T) * J, LANES), f32), vmem((G, (KW + 1) * J, LANES), f32),
            vmem((G, T, GW), bf16), vmem((T * N, LANES), f32), vmem((T * N, LANES), f32), vmem((G, N * J, LANES), f32),
            vmem((T, R + 2 * N), f32), vmem((G // 2 + 1, ROWS, LANES), f32), vmem((G // 2 + 1, ROWS, LANES), f32),
            vmem((G, ROWS, LANES), f32), vmem((G // 2, ROWS, LANES), f32), vmem((G, T, GW), f32),
            vmem((C * 8 * AGG, LANES), f32), vmem((C * 8 * AGG, LANES), f32), vmem((C * WIRE, LANES), bf16),
            vmem((C * 16 * WIRE, LANES), bf16), vmem((C * 8 * 2 * N, LANES), f32), vmem((C * 8 * 2 * N, LANES), f32),
            dma((3, G)), dma((5,)), dma((G,)), dma((G,)), dma((G,)),
            dma((C, 8)), dma((C, 8)), dma((C, 16)), dma((C, 16)), dma((C, 8)), dma((C, 8))],
        compiler_params=pltpu.CompilerParams(collective_id=0, has_side_effects=True, vmem_limit_bytes=52 * 2**20),
    )(*(pltpu.with_memory_space_constraint(v, pltpu.HBM) for v in (
        x_in, conv_weight, conv_bias.reshape(1, E), x_proj.T, dt_proj, dt_bias.reshape(1, E), decay_rates,
        skip_gain.reshape(1, E))))
    gate = gate_in.astype(f32)
    return (y * (gate * (0.5 * jnp.tanh(0.5 * gate) + 0.5))).astype(bf16)


def solution(mesh):
    tokens = P(("outer", "inner"), None)
    return jax.shard_map(
        local, mesh=mesh, in_specs=(tokens, tokens, P(), P(), P(), P(), P(), P(), P()),
        out_specs=tokens, check_vma=False)
```
